32 devices in a mesh: rows: 8 (over y, x, core), vecs: 4 (over z).
Axes of the slice: x: 2, y: 2, z: 4, core: 2. Of those that a mesh axis runs over, the one named last changes fastest.
Arguments:
- vectors: float32 [1024, 512], P('rows', 'vecs'), may hold values from -6 to 6
- reflectors: float32 [3, 8, 128, 256], P(None, 'rows', 'vecs'), may hold values from -3 to 3
Outputs:
- transformed: float32 [1024, 512], P('rows', 'vecs')
The draws below stay inside these ranges and needn't reach their ends.
All inputs are finite; a program needn't handle non-finite values.
Results may differ from the reference program's by a relative error of at most 0.0003.
Values sent between devices are 32-bit elements; how exact they have to be, the bound alone decides.
No kernel may reach another device: no remote copies, remote signals or barrier semaphores. Data moves between devices by JAX's collectives and lax.ppermute only.
A program may use at most 64 MiB of HBM per device.

```python
import math
import jax
import jax.numpy as jnp
from jax import lax

KB = 128
GROUPS = 3
NROWS = 1024
NVECS = 512
NBLK = 8


def draw_reflectors(key, part):
    basis_key = jax.random.fold_in(key, 23)
    noise_key = jax.random.fold_in(key, 11)
    scale_key = jax.random.fold_in(key, 37)
    gaussian = jax.random.normal(basis_key, (GROUPS, NBLK, KB, KB), jnp.float32)
    orthogonal = jnp.linalg.qr(gaussian)[0]
    identity = jnp.broadcast_to(jnp.eye(KB, dtype=jnp.float32), orthogonal.shape)
    pattern = jnp.concatenate([identity, -orthogonal], 3)
    spread = 0.05 / math.sqrt(KB)
    jitter = jnp.clip(jax.random.normal(noise_key, pattern.shape, jnp.float32), -4.0, 4.0) * spread
    log_scale = jax.random.uniform(scale_key, (GROUPS, NBLK, KB, 1), jnp.float32, math.log(0.5), math.log(2.0))
    return jnp.exp(log_scale) * (pattern + jitter)


def levels(key, dims, shards, least, top_value):
    gain, own = 1.0, jax.random.fold_in(key, 6)
    for dim, shards_of in shards:
        draws = jnp.exp(jax.random.uniform(jax.random.fold_in(own, dim), (shards_of,), jnp.float32, least / len(shards), top_value / len(shards)))
        gain = gain * jnp.repeat(draws, dims[dim] // shards_of).reshape([-1 if axis == dim else 1 for axis in range(len(dims))])
    return gain


def normal_values(own_key, shape, deviation, reach, cuts=(), kind=jnp.bfloat16):
    gain = levels(own_key, shape, cuts, -0.22, 0.18) if cuts else 1.0
    values = jax.random.normal(own_key, shape, jnp.float32) * deviation * gain
    return jnp.minimum(jnp.maximum(values, -reach), reach).astype(kind)


def setup_inputs(seed: int = 0) -> dict:
    key_list = jax.random.split(jax.random.key(seed), 3)
    return {
        "vectors": normal_values(key_list[0], (NROWS, NVECS), 1.0, 6.0, ((0, 8), (1, 4)), jnp.float32),
        "reflectors": draw_reflectors(jax.random.fold_in(key_list[2], 71), 0),
    }


HIGHEST = lax.Precision.HIGHEST

def factor(reflector):
    gram_matrix = jnp.dot(reflector, reflector.T, precision=HIGHEST)
    return jnp.triu(gram_matrix, 1) + jnp.diag(jnp.diag(gram_matrix)) * 0.5

def reflect(window_rows, reflector, inv_factor):
    weights = jnp.dot(reflector, window_rows, precision=HIGHEST)
    solved = lax.linalg.triangular_solve(inv_factor, weights, left_side=True, lower=False)
    return window_rows - jnp.dot(reflector.T, solved, precision=HIGHEST)

def reference(vectors, reflectors):
    block_size = reflectors.shape[2]
    block_count = reflectors.shape[1]
    row_pos = lax.broadcasted_iota(jnp.int32, reflectors.shape, 3)
    block_pos = lax.broadcasted_iota(jnp.int32, reflectors.shape, 1)
    masked = jnp.where((block_pos == block_count - 1) & (row_pos >= block_size), jnp.zeros_like(reflectors), reflectors)
    padded = jnp.concatenate([vectors, jnp.zeros((block_size, vectors.shape[1]), vectors.dtype)], 0)
    for group in range(GROUPS):
        group_blocks = masked[group]

        def advance(block, state):
            block_index = jnp.asarray(block).astype(jnp.int32)
            reflector = lax.dynamic_index_in_dim(group_blocks, block_index, 0, keepdims=False)
            start_row = (block_index * block_size).astype(jnp.int32)
            window_rows = lax.dynamic_slice_in_dim(state, start_row, 2 * block_size, 0)
            updated = reflect(window_rows, reflector, factor(reflector))
            return lax.dynamic_update_slice_in_dim(state, updated, start_row, 0)
        padded = lax.fori_loop(0, block_count, advance, padded)
    return padded[:NROWS]
```

```python
import jax
import jax.numpy as jnp
from jax import lax
from jax.sharding import PartitionSpec as P

HIGHEST = lax.Precision.HIGHEST
PAIR = 2


def dot(left, right):
    return jnp.matmul(left, right, precision=HIGHEST)


def spread(value, axis, index, size):
    if size & (size - 1) or size > 8:
        gathered = lax.all_gather(value, axis)
        return [gathered[place] for place in range(size)]
    order = [value]
    for mask in range(1, size):
        order.append(lax.ppermute(value, axis, [(place, place ^ mask) for place in range(size)]))
    bit = 1
    while bit < size:
        flip = (index & bit) != 0
        order = [jnp.where(flip, order[place ^ bit], order[place]) for place in range(size)]
        bit *= 2
    return order


def block_mask(size, block):
    row = lax.broadcasted_iota(jnp.int32, (size, size), 0)
    col = lax.broadcasted_iota(jnp.int32, (size, size), 1)
    return (row // block) == (col // block)


def unit_upper_inverse(strict):
    size = strict.shape[-1]
    eye = jnp.eye(size, dtype=strict.dtype)
    block = min(8, size)
    near = jnp.where(block_mask(size, block), strict, 0.0)
    square = dot(near, near)
    fourth = dot(square, square)
    result = eye - near
    result = result + dot(result, square)
    result = result + dot(result, fourth)
    while block < size:
        step = 4 if 4 * block <= size else 2
        ring = block_mask(size, block * step) & ~block_mask(size, block)
        across = dot(result, jnp.where(ring, strict, 0.0))
        once = result - dot(across, result)
        if step == 4:
            once = once + dot(dot(across, across), once)
        result = once
        block *= step
    return result


def pair_operators(first, second):
    groups, block, _ = first.shape
    none = jnp.zeros((groups, block, block), first.dtype)
    joined = jnp.concatenate(
        [jnp.concatenate([none, second], 2), jnp.concatenate([first, none], 2)], 1
    )
    gram = jnp.einsum("gik,gjk->gij", joined, joined, precision=HIGHEST)
    size = 2 * block
    row = lax.broadcasted_iota(jnp.int32, (size, size), 0)
    col = lax.broadcasted_iota(jnp.int32, (size, size), 1)
    half_diag = 0.5 * jnp.sum(jnp.where(row == col, gram, 0.0), 2)
    strict = jnp.where(row < col, gram, 0.0) / half_diag[:, :, None]
    inverse = unit_upper_inverse(strict) / half_diag[:, None, :]
    solved = dot(inverse, joined)
    reached = jnp.einsum("gki,gkj->gij", joined, solved, precision=HIGHEST)
    return jnp.eye(3 * block, dtype=first.dtype) - reached


def local(vectors, reflectors):
    groups, _, _, window = reflectors.shape
    block = window // 2
    row_index = lax.axis_index("rows")
    row_count = lax.axis_size("rows")
    vec_index = lax.axis_index("vecs")
    vec_count = lax.axis_size("vecs")
    nodes = row_count // PAIR
    node = row_index // PAIR
    upper = (row_index % PAIR) == 0
    is_first = node == 0
    is_last = node == nodes - 1
    other_core = [(place, place ^ 1) for place in range(row_count)]

    def both(mine):
        theirs = lax.ppermute(mine, "rows", other_core)
        return jnp.where(upper, mine, theirs), jnp.where(upper, theirs, mine)

    top, low = both(vectors)
    below = lax.ppermute(
        top, "rows", [(place, place - PAIR) for place in range(PAIR, row_count)]
    )
    mine = jnp.concatenate(spread(reflectors[:, 0], "vecs", vec_index, vec_count), 1)
    first, second = both(mine)
    col = lax.broadcasted_iota(jnp.int32, second.shape, 2)
    second = jnp.where(is_last & (col >= block), 0.0, second)
    operators = pair_operators(first, second)

    def exchange(down, up, want_up):
        if nodes & (nodes - 1) or nodes > 4:
            members = [
                [place * PAIR + core for place in range(nodes)] for core in range(PAIR)
            ]
            earlier = lax.all_gather(down, "rows", axis_index_groups=members)
            earlier = [earlier[place] for place in range(nodes - 1)]
            later = lax.ppermute(
                up, "rows", [(place, place - PAIR) for place in range(PAIR, row_count)]
            )
            return earlier, later
        came = {}
        for mask in range(1, nodes):
            moves = [
                (place, place ^ mask)
                for place in range(nodes)
                if place ^ mask > place or (want_up and place ^ mask == place - 1)
            ]
            value = jnp.where((node ^ mask) > node, down, up) if want_up else down
            came[mask] = lax.ppermute(
                value,
                "rows",
                [
                    (source * PAIR + core, target * PAIR + core)
                    for source, target in moves
                    for core in range(PAIR)
                ],
            )
        earlier = []
        for place in range(nodes - 1):
            value = came[1]
            for mask in range(2, nodes):
                value = jnp.where((node ^ place) == mask, came[mask], value)
            earlier.append(value)
        later = came[1]
        for mask in range(2, nodes):
            later = jnp.where((node ^ (node + 1)) == mask, came[mask], later)
        return earlier, later

    for group in range(groups):
        operator = operators[group]
        last_group = group == groups - 1
        window_rows = jnp.concatenate(
            [jnp.where(is_first, top, 0.0), low, jnp.where(is_last, 0.0, below)], 0
        )
        fixed = dot(operator, window_rows)
        lead = operator[:, :block]
        down = jnp.concatenate([fixed[2 * block :], lead[2 * block :]], 0)
        up = jnp.concatenate([fixed[:block], lead[:block]], 0)
        earlier, later = exchange(down, up, not last_group)
        carry = jnp.zeros_like(top)
        for place, value in enumerate(earlier):
            if place == 0:
                step = value[:block]
            else:
                step = value[:block] + dot(value[block:], carry)
            carry = jnp.where(node > place, step, carry)
        result = fixed + dot(lead, carry)
        top = result[:block]
        low = result[block : 2 * block]
        if not last_group:
            below = later[:block] + dot(later[block:], result[2 * block :])
    return jnp.where(upper, top, low)


def solution(mesh):
    placed = (P("rows", "vecs"), P(None, "rows", "vecs", None))
    return jax.shard_map(
        local, mesh=mesh, in_specs=placed, out_specs=P("rows", "vecs"), check_vma=False
    )
```

```python
import jax
import jax.numpy as jnp
from jax import lax
from jax.experimental import pallas as pl
from jax.experimental.pallas import tpu as pltpu
from jax.sharding import PartitionSpec as P

PAIR = 2
F32, BF16 = jnp.float32, jnp.bfloat16
NN = ((1,), (0,))
NT = ((1,), (1,))
TN = ((0,), (0,))


def halves(value):
    high = value.astype(BF16)
    return high, (value - high.astype(F32)).astype(BF16)


def mm(left, right, dims=NN):
    left = left if isinstance(left, tuple) else halves(left)
    right = right if isinstance(right, tuple) else halves(right)

    def one(a, b):
        return lax.dot_general(a, b, (dims, ((), ())), preferred_element_type=F32)

    return one(left[0], right[0]) + (one(left[0], right[1]) + one(left[1], right[0]))


def same_block(shape, rows_block, cols_block, wrap):
    row = lax.broadcasted_iota(jnp.int32, shape, 0)
    col = lax.broadcasted_iota(jnp.int32, shape, 1)
    return (row // rows_block) == ((col % wrap) // cols_block)


def operators_kernel(flag_ref, first_ref, second_ref, out_ref):
    groups, block, window = first_ref.shape
    wide = 2 * block
    groups = range(groups)
    keep = flag_ref[0] == 0
    firsts, seconds, sfirst, ssecond = [], [], [], []
    col = lax.broadcasted_iota(jnp.int32, (block, window), 1)
    for g in groups:
        a = first_ref[g]
        b = jnp.where(keep | (col < block), second_ref[g], 0.0)
        firsts.append(a)
        seconds.append(b)
        sfirst.append(a * (2.0 / jnp.sum(a * a, 1, keepdims=True)))
        ssecond.append(b * (2.0 / jnp.sum(b * b, 1, keepdims=True)))
    above = lax.broadcasted_iota(jnp.int32, (block, wide), 0) < (
        lax.broadcasted_iota(jnp.int32, (block, wide), 1) % block
    )
    near, cross = [], []
    for g in groups:
        ha = halves(firsts[g])
        gq = mm(ssecond[g], halves(seconds[g]), NT)
        gp = mm(sfirst[g], ha, NT)
        near.append(jnp.where(above, jnp.concatenate([gq, gp], 1), 0.0))
        cross.append(
            mm(ssecond[g][:, :block], (ha[0][:, block:], ha[1][:, block:]), NT)
        )

    def diagonal(value, size):
        mask = same_block((wide, wide), size, size, wide)
        return tuple(
            jnp.where(mask, jnp.concatenate([part] * (wide // size), 0), jnp.zeros((), BF16))
            for part in halves(value)
        )

    def gather_blocks(value, size):
        total = None
        for place in range(block // size):
            part = value[place * size : (place + 1) * size]
            pcol = lax.broadcasted_iota(jnp.int32, part.shape, 1)
            part = jnp.where((pcol % block) // size == place, part, 0.0)
            total = part if total is None else total + part
        return total

    def widen(value, size):
        old = value.shape[0]
        tall = jnp.concatenate([value] * (size // old), 0)
        return jnp.where(same_block(tall.shape, old, old, size), tall, 0.0)

    def quad(result, ring, size):
        across = [mm(r, diagonal(b, size)) for r, b in zip(result, ring)]
        halved = [halves(x) for x in across]
        once = [r - mm(x, diagonal(r, size)) for r, x in zip(result, halved)]
        square = [mm(h, diagonal(x, size)) for h, x in zip(halved, across)]
        return [o + mm(s, diagonal(o, size)) for o, s in zip(once, square)]

    small = [gather_blocks(n, 16) for n in near]
    shape = small[0].shape
    row = lax.broadcasted_iota(jnp.int32, shape, 0)
    scol = lax.broadcasted_iota(jnp.int32, shape, 1)
    eye = jnp.where(row == scol % 16, 1.0, 0.0)
    inner = (row // 4) == (scol % 16) // 4
    tiny = [jnp.where(inner, n, 0.0) for n in small]
    square = [mm(n, diagonal(n, 16)) for n in tiny]
    result = [eye - n for n in tiny]
    result = [r + mm(r, diagonal(s, 16)) for r, s in zip(result, square)]
    result = quad(result, [jnp.where(inner, 0.0, n) for n in small], 16)
    middle = [gather_blocks(n, 64) for n in near]
    mmask = same_block(middle[0].shape, 16, 16, 64)
    result = [widen(r, 64) for r in result]
    result = quad(result, [jnp.where(mmask, 0.0, n) for n in middle], 64)
    result = [widen(r, block) for r in result]
    bmask = same_block((block, wide), 64, 64, block)
    across = [mm(r, diagonal(jnp.where(bmask, 0.0, n), block)) for r, n in zip(result, near)]
    result = [r - mm(x, diagonal(r, block)) for r, x in zip(result, across)]
    for g in groups:
        q, p = halves(result[g][:, :block]), halves(result[g][:, block:])
        link = mm(q, cross[g])
        link = mm(link, p)
        solved_p = mm(p, sfirst[g])
        low = halves(sfirst[g])
        solved_q = mm(q, ssecond[g])
        reach = mm(link, low)
        zero = jnp.zeros((block, block), F32)
        sq = jnp.concatenate([-reach[:, :block], solved_q[:, :block] - reach[:, block:], solved_q[:, block:]], 1)
        sp = jnp.concatenate([solved_p, zero], 1)
        solved = jnp.concatenate([sq, sp], 0)
        joined = jnp.concatenate(
            [
                jnp.concatenate([zero, seconds[g]], 1),
                jnp.concatenate([firsts[g], zero], 1),
            ],
            0,
        )
        moved = mm(joined, solved, TN)
        orow = lax.broadcasted_iota(jnp.int32, moved.shape, 0)
        ocol = lax.broadcasted_iota(jnp.int32, moved.shape, 1)
        out_ref[g] = jnp.where(orow == ocol, 1.0, 0.0) - moved


def pair_operators(first, second, is_last):
    groups, block, _ = first.shape
    return pl.pallas_call(
        operators_kernel,
        out_shape=jax.ShapeDtypeStruct((groups, 3 * block, 3 * block), F32),
        in_specs=[
            pl.BlockSpec(memory_space=pltpu.SMEM),
            pl.BlockSpec(memory_space=pltpu.VMEM),
            pl.BlockSpec(memory_space=pltpu.VMEM),
        ],
        out_specs=pl.BlockSpec(memory_space=pltpu.VMEM),
        compiler_params=pltpu.CompilerParams(vmem_limit_bytes=32 << 20),
    )(is_last.astype(jnp.int32).reshape(1), first, second)


def dot(left, right):
    return jnp.matmul(left, right, precision=lax.Precision.HIGHEST)


def spread(value, axis, index, size):
    if size & (size - 1) or size > 8:
        gathered = lax.all_gather(value, axis)
        return [gathered[place] for place in range(size)]
    order = [value]
    for mask in range(1, size):
        order.append(lax.ppermute(value, axis, [(place, place ^ mask) for place in range(size)]))
    bit = 1
    while bit < size:
        flip = (index & bit) != 0
        order = [jnp.where(flip, order[place ^ bit], order[place]) for place in range(size)]
        bit *= 2
    return order


def local(vectors, reflectors):
    groups, _, _, window = reflectors.shape
    block = window // 2
    row_index = lax.axis_index("rows")
    row_count = lax.axis_size("rows")
    vec_index = lax.axis_index("vecs")
    vec_count = lax.axis_size("vecs")
    nodes = row_count // PAIR
    node = row_index // PAIR
    upper = (row_index % PAIR) == 0
    is_first = node == 0
    is_last = node == nodes - 1

    def swap(value, masks):
        moves = [
            (place, ((place // PAIR) ^ masks[place % PAIR]) * PAIR + place % PAIR)
            for place in range(row_count)
        ]
        return lax.ppermute(value, "rows", moves)

    def across(value):
        return lax.ppermute(value, "rows", [(place, place ^ 1) for place in range(row_count)])

    def both(mine):
        theirs = across(mine)
        return jnp.where(upper, mine, theirs), jnp.where(upper, theirs, mine)

    def exchange(down, up, want_up):
        if nodes != 4:
            members = [
                [place * PAIR + core for place in range(nodes)] for core in range(PAIR)
            ]
            earlier = lax.all_gather(down, "rows", axis_index_groups=members)
            earlier = [earlier[place] for place in range(nodes - 1)]
            later = lax.ppermute(
                up, "rows", [(place, place - PAIR) for place in range(PAIR, row_count)]
            )
            return earlier, later
        near = swap(
            jnp.where(upper & ((node & 1) == 1), up, down) if want_up else down, (1, 2)
        )
        low_half = (node & 2) == 0
        far = swap(
            jnp.where(
                upper,
                jnp.where(low_half, down[:block], up[:block]),
                jnp.where(low_half, down[block:], up[block:]),
            ),
            (3, 3),
        )
        near_other = across(near)
        far_other = across(far)
        came = {
            1: jnp.where(upper, near, near_other),
            2: jnp.where(upper, near_other, near),
            3: jnp.concatenate(
                [jnp.where(upper, far, far_other), jnp.where(upper, far_other, far)], 0
            ),
        }
        earlier = []
        for place in range(nodes - 1):
            value = came[1]
            for mask in range(2, nodes):
                value = jnp.where((node ^ place) == mask, came[mask], value)
            earlier.append(value)
        later = came[1]
        for mask in range(2, nodes):
            later = jnp.where((node ^ (node + 1)) == mask, came[mask], later)
        return earlier, later

    top, low = both(vectors)
    if nodes == 4:
        below = jnp.where((node & 1) == 0, swap(top, (1, 1)), swap(top, (3, 3)))
    else:
        below = lax.ppermute(
            top, "rows", [(place, place - PAIR) for place in range(PAIR, row_count)]
        )
    mine = jnp.concatenate(spread(reflectors[:, 0], "vecs", vec_index, vec_count), 1)
    mine, below = lax.optimization_barrier((mine, below))
    first, second = both(mine)
    operators = pair_operators(first, second, is_last)

    for group in range(groups):
        operator = operators[group]
        last_group = group == groups - 1
        window_rows = jnp.concatenate(
            [jnp.where(is_first, top, 0.0), low, jnp.where(is_last, 0.0, below)], 0
        )
        fixed = dot(operator, window_rows)
        lead = operator[:, :block]
        down = jnp.concatenate([fixed[2 * block :], lead[2 * block :]], 0)
        up = jnp.concatenate([fixed[:block], lead[:block]], 0)
        earlier, later = exchange(down, up, not last_group)
        carry = jnp.zeros_like(top)
        for place, value in enumerate(earlier):
            if place == 0:
                step = value[:block]
            else:
                step = value[:block] + dot(value[block:], carry)
            carry = jnp.where(node > place, step, carry)
        result = fixed + dot(lead, carry)
        top = result[:block]
        low = result[block : 2 * block]
        if not last_group:
            below = later[:block] + dot(later[block:], result[2 * block :])
    return jnp.where(upper, top, low)


def solution(mesh):
    placed = (P("rows", "vecs"), P(None, "rows", "vecs", None))
    return jax.shard_map(
        local, mesh=mesh, in_specs=placed, out_specs=P("rows", "vecs"), check_vma=False
    )
```

```python
import functools
import jax
import jax.numpy as jnp
from jax import lax
from jax.experimental import pallas as pl
from jax.experimental.pallas import tpu as pltpu
from jax.sharding import PartitionSpec as P

PAIR = 2
F32, BF16 = jnp.float32, jnp.bfloat16
NN = ((1,), (0,))
NT = ((1,), (1,))
TN = ((0,), (0,))


def halves(value):
    high = value.astype(BF16)
    return high, (value - high.astype(F32)).astype(BF16)


def mm(left, right, dims=NN):
    left = left if isinstance(left, tuple) else halves(left)
    right = right if isinstance(right, tuple) else halves(right)

    (lc,), (rc,) = dims
    return lax.dot_general(
        jnp.concatenate([left[0], left[0], left[1]], lc),
        jnp.concatenate([right[0], right[1], right[0]], rc),
        (dims, ((), ())),
        preferred_element_type=F32,
    )


def same_block(shape, rows_block, cols_block, wrap):
    row = lax.broadcasted_iota(jnp.int32, shape, 0)
    col = lax.broadcasted_iota(jnp.int32, shape, 1)
    return (row // rows_block) == ((col % wrap) // cols_block)


def pair_operators(refl_ref, keep, out_ref):
    _, groups, block, window = refl_ref.shape
    wide = 2 * block
    groups = range(groups)
    firsts, seconds, sfirst, ssecond = [], [], [], []
    col = lax.broadcasted_iota(jnp.int32, (block, window), 1)
    for g in groups:
        a = refl_ref[0, g]
        b = jnp.where(keep | (col < block), refl_ref[1, g], 0.0)
        firsts.append(a)
        seconds.append(b)
        sfirst.append(a * (2.0 / jnp.sum(a * a, 1, keepdims=True)))
        ssecond.append(b * (2.0 / jnp.sum(b * b, 1, keepdims=True)))
    above = lax.broadcasted_iota(jnp.int32, (block, wide), 0) < (
        lax.broadcasted_iota(jnp.int32, (block, wide), 1) % block
    )
    near, cross = [], []
    for g in groups:
        ha = halves(firsts[g])
        gq = mm(ssecond[g], halves(seconds[g]), NT)
        gp = mm(sfirst[g], ha, NT)
        near.append(jnp.where(above, jnp.concatenate([gq, gp], 1), 0.0))
        cross.append(
            mm(ssecond[g][:, :block], (ha[0][:, block:], ha[1][:, block:]), NT)
        )

    def diagonal(value, size):
        mask = same_block((wide, wide), size, size, wide)
        return tuple(
            jnp.where(mask, jnp.concatenate([part] * (wide // size), 0), jnp.zeros((), BF16))
            for part in halves(value)
        )

    def gather_blocks(value, size):
        total = None
        for place in range(block // size):
            part = value[place * size : (place + 1) * size]
            pcol = lax.broadcasted_iota(jnp.int32, part.shape, 1)
            part = jnp.where((pcol % block) // size == place, part, 0.0)
            total = part if total is None else total + part
        return total

    def widen(value, size):
        old = value.shape[0]
        tall = jnp.concatenate([value] * (size // old), 0)
        return jnp.where(same_block(tall.shape, old, old, size), tall, 0.0)

    def quad(result, ring, size):
        across = [mm(r, diagonal(b, size)) for r, b in zip(result, ring)]
        halved = [halves(x) for x in across]
        once = [r - mm(x, diagonal(r, size)) for r, x in zip(result, halved)]
        square = [mm(h, diagonal(x, size)) for h, x in zip(halved, across)]
        return [o + mm(s, diagonal(o, size)) for o, s in zip(once, square)]

    small = [gather_blocks(n, 16) for n in near]
    shape = small[0].shape
    row = lax.broadcasted_iota(jnp.int32, shape, 0)
    scol = lax.broadcasted_iota(jnp.int32, shape, 1)
    eye = jnp.where(row == scol % 16, 1.0, 0.0)
    inner = (row // 4) == (scol % 16) // 4
    tiny = [jnp.where(inner, n, 0.0) for n in small]
    square = [mm(n, diagonal(n, 16)) for n in tiny]
    result = [eye - n for n in tiny]
    result = [r + mm(r, diagonal(s, 16)) for r, s in zip(result, square)]
    result = quad(result, [jnp.where(inner, 0.0, n) for n in small], 16)
    middle = [gather_blocks(n, 64) for n in near]
    mmask = same_block(middle[0].shape, 16, 16, 64)
    result = [widen(r, 64) for r in result]
    result = quad(result, [jnp.where(mmask, 0.0, n) for n in middle], 64)
    result = [widen(r, block) for r in result]
    bmask = same_block((block, wide), 64, 64, block)
    across = [mm(r, diagonal(jnp.where(bmask, 0.0, n), block)) for r, n in zip(result, near)]
    result = [r - mm(x, diagonal(r, block)) for r, x in zip(result, across)]
    for g in groups:
        q, p = halves(result[g][:, :block]), halves(result[g][:, block:])
        link = mm(q, cross[g])
        link = mm(link, p)
        solved_p = mm(p, sfirst[g])
        low = halves(sfirst[g])
        solved_q = mm(q, ssecond[g])
        reach = mm(link, low)
        zero = jnp.zeros((block, block), F32)
        sq = jnp.concatenate([-reach[:, :block], solved_q[:, :block] - reach[:, block:], solved_q[:, block:]], 1)
        sp = jnp.concatenate([solved_p, zero], 1)
        solved = jnp.concatenate([sq, sp], 0)
        joined = jnp.concatenate(
            [
                jnp.concatenate([zero, seconds[g]], 1),
                jnp.concatenate([firsts[g], zero], 1),
            ],
            0,
        )
        moved = mm(joined, solved, TN)
        orow = lax.broadcasted_iota(jnp.int32, moved.shape, 0)
        ocol = lax.broadcasted_iota(jnp.int32, moved.shape, 1)
        out_ref[g] = jnp.where(orow == ocol, 1.0, 0.0) - moved


def payloads(node, core, fixed, lead, near_ref, far_ref):
    block = lead.shape[1]
    up, down = slice(0, block), slice(2 * block, None)
    send_up = (core == 0) & ((node & 1) == 1)
    near_ref[:block] = jnp.where(send_up, fixed[up], fixed[down])
    near_ref[block:] = jnp.where(send_up, lead[up], lead[down])
    low_half = (node & 2) == 0
    far_ref[...] = jnp.where(
        core == 0,
        jnp.where(low_half, fixed[down], fixed[up]),
        jnp.where(low_half, lead[down], lead[up]),
    )


def first_kernel(count, nodes, place_ref, *refs):
    mine, theirs = refs[:count], refs[count : 2 * count]
    own_ref, other_ref, near_ref, far_ref = refs[2 * count : 2 * count + 4]
    oper_ref, fixed_ref, out_near, out_far, refl_ref = refs[2 * count + 4 :]
    block = own_ref.shape[0]
    node, core, vec = place_ref[0], place_ref[1], place_ref[2]
    groups, rows, _ = mine[0].shape
    for step in range(count):
        at = pl.ds(pl.multiple_of((step ^ vec) * rows, rows), rows)
        for group in range(groups):
            refl_ref[core, group, at, :] = mine[step][group]
            refl_ref[1 - core, group, at, :] = theirs[step][group]
    pair_operators(refl_ref, node != nodes - 1, oper_ref)
    own, other = own_ref[...], other_ref[...]
    top = jnp.where(core == 0, own, other)
    low = jnp.where(core == 0, other, own)
    below = jnp.where((node & 1) == 0, near_ref[...], far_ref[...])
    window = jnp.concatenate(
        [
            jnp.where(node == 0, top, 0.0),
            low,
            jnp.where(node == nodes - 1, 0.0, below),
        ],
        0,
    )
    fixed = mm(oper_ref[0], window)
    fixed_ref[...] = fixed
    payloads(node, core, fixed, oper_ref[0, :, :block], out_near, out_far)


def next_kernel(group, place_ref, near_ref, far_ref, near2_ref, far2_ref, fixed_ref, oper_ref, *outs):
    block = far_ref.shape[0]
    node, core = place_ref[0], place_ref[1]
    here = core == 0
    near, near2, far, far2 = near_ref[...], near2_ref[...], far_ref[...], far2_ref[...]
    came1 = jnp.where(here, near, near2)
    came2 = jnp.where(here, near2, near)
    came3 = jnp.where(here, far, far2), jnp.where(here, far2, far)
    odd, high = (node & 1) == 1, (node & 2) == 2
    carry = jnp.where(high, jnp.where(odd, came3[0], came2[:block]), came1[:block])
    carry = jnp.where(node == 0, 0.0, carry)
    step = jnp.where(odd, came2[:block], came3[0]) + mm(
        jnp.where(odd, came2[block:], came3[1]), carry
    )
    carry = jnp.where(high, step, carry)
    step = came1[:block] + mm(came1[block:], carry)
    carry = jnp.where(node == 3, step, carry)
    result = fixed_ref[...] + mm(oper_ref[group, :, :block], carry)
    top, low, out = result[:block], result[block : 2 * block], result[2 * block :]
    if len(outs) == 1:
        outs[0][...] = jnp.where(here, top, low)
        return
    below = jnp.where(odd, came3[0], came1[:block]) + mm(
        jnp.where(odd, came3[1], came1[block:]), out
    )
    window = jnp.concatenate(
        [jnp.where(node == 0, top, 0.0), low, jnp.where(node == 3, 0.0, below)], 0
    )
    fixed = mm(oper_ref[group + 1], window)
    outs[0][...] = fixed
    payloads(node, core, fixed, oper_ref[group + 1, :, :block], outs[1], outs[2])


def call(kernel, outs, operands, scratch=()):
    vmem = pl.BlockSpec(memory_space=pltpu.VMEM)
    return pl.pallas_call(
        kernel,
        out_shape=[jax.ShapeDtypeStruct(shape, F32) for shape in outs],
        in_specs=[pl.BlockSpec(memory_space=pltpu.SMEM)] + [vmem] * (len(operands) - 1),
        out_specs=[vmem] * len(outs),
        scratch_shapes=list(scratch),
        compiler_params=pltpu.CompilerParams(vmem_limit_bytes=16 << 20),
    )(*operands)


def dot(left, right):
    return jnp.matmul(left, right, precision=lax.Precision.HIGHEST)


def spread(value, axis, size):
    if size & (size - 1) or size > 8:
        gathered = lax.all_gather(value, axis)
        return [gathered[place] for place in range(size)], False
    return [value] + [
        lax.ppermute(value, axis, [(place, place ^ mask) for place in range(size)])
        for mask in range(1, size)
    ], True


def many_pairs(fixed, operators, node, nodes, row_count):
    groups, _, block = operators.shape[0], None, operators.shape[1] // 3
    members = [[place * PAIR + core for place in range(nodes)] for core in range(PAIR)]
    for group in range(groups):
        lead = operators[group][:, :block]
        down = jnp.concatenate([fixed[2 * block :], lead[2 * block :]], 0)
        up = jnp.concatenate([fixed[:block], lead[:block]], 0)
        earlier = lax.all_gather(down, "rows", axis_index_groups=members)
        later = lax.ppermute(
            up, "rows", [(place, place - PAIR) for place in range(PAIR, row_count)]
        )
        carry = jnp.zeros((block, fixed.shape[1]), F32)
        for place in range(nodes - 1):
            step = earlier[place, :block] + dot(earlier[place, block:], carry)
            carry = jnp.where(node > place, step, carry)
        result = fixed + dot(lead, carry)
        if group < groups - 1:
            below = later[:block] + dot(later[block:], result[2 * block :])
            window = jnp.concatenate(
                [
                    jnp.where(node == 0, result[:block], 0.0),
                    result[block : 2 * block],
                    jnp.where(node == nodes - 1, 0.0, below),
                ],
                0,
            )
            fixed = dot(operators[group + 1], window)
    return result


def local(vectors, reflectors):
    groups, _, _, window = reflectors.shape
    block = window // 2
    cols = vectors.shape[1]
    row_index = lax.axis_index("rows")
    row_count = lax.axis_size("rows")
    vec_index = lax.axis_index("vecs")
    vec_count = lax.axis_size("vecs")
    nodes = row_count // PAIR
    node = row_index // PAIR
    core = row_index % PAIR

    def swap(value, masks):
        moves = [
            (place, ((place // PAIR) ^ masks[place % PAIR]) * PAIR + place % PAIR)
            for place in range(row_count)
        ]
        return lax.ppermute(value, "rows", moves)

    def across(value):
        return lax.ppermute(value, "rows", [(place, place ^ 1) for place in range(row_count)])

    mine, mixed = spread(reflectors[:, 0], "vecs", vec_count)
    other = across(vectors)
    top = jnp.where(core == 0, vectors, other)
    if nodes == 4:
        below = [swap(top, (1, 1)), swap(top, (3, 3))]
    else:
        below = [
            lax.ppermute(
                top, "rows", [(place, place - PAIR) for place in range(PAIR, row_count)]
            )
        ] * 2
    theirs = [across(piece) for piece in mine]
    place = jnp.stack([node, core, vec_index if mixed else 0]).astype(jnp.int32)
    operators, fixed, near, far = call(
        functools.partial(first_kernel, len(mine), nodes),
        [
            (groups, 3 * block, 3 * block),
            (3 * block, cols),
            (2 * block, cols),
            (block, cols),
        ],
        [place, *mine, *theirs, vectors, other, *below],
        [pltpu.VMEM((PAIR, groups, block, window), F32)],
    )
    if nodes != 4:
        result = many_pairs(fixed, operators, node, nodes, row_count)
        return jnp.where(core == 0, result[:block], result[block : 2 * block])
    for group in range(groups):
        near = swap(near, (1, 2))
        far = swap(far, (3, 3))
        operands = [place, near, far, across(near), across(far), fixed, operators]
        if group < groups - 1:
            fixed, near, far = call(
                functools.partial(next_kernel, group),
                [(3 * block, cols), (2 * block, cols), (block, cols)],
                operands,
            )
        else:
            (result,) = call(
                functools.partial(next_kernel, group), [(block, cols)], operands
            )
    return result


def solution(mesh):
    placed = (P("rows", "vecs"), P(None, "rows", "vecs", None))
    return jax.shard_map(
        local, mesh=mesh, in_specs=placed, out_specs=P("rows", "vecs"), check_vma=False
    )
```

```python
import functools
import jax
import jax.numpy as jnp
from jax import lax
from jax.experimental import pallas as pl
from jax.experimental.pallas import tpu as pltpu
from jax.sharding import PartitionSpec as P

PAIR = 2
F32, BF16 = jnp.float32, jnp.bfloat16
NN = ((1,), (0,))
NT = ((1,), (1,))
TN = ((0,), (0,))


def halves(value):
    high = value.astype(BF16)
    return high, (value - high.astype(F32)).astype(BF16)


def mm(left, right, dims=NN):
    left = left if isinstance(left, tuple) else halves(left)
    right = right if isinstance(right, tuple) else halves(right)

    (lc,), (rc,) = dims
    return lax.dot_general(
        jnp.concatenate([left[0], left[0], left[1]], lc),
        jnp.concatenate([right[0], right[1], right[0]], rc),
        (dims, ((), ())),
        preferred_element_type=F32,
    )


def same_block(shape, rows_block, cols_block, wrap):
    row = lax.broadcasted_iota(jnp.int32, shape, 0)
    col = lax.broadcasted_iota(jnp.int32, shape, 1)
    return (row // rows_block) == ((col % wrap) // cols_block)


def pair_operators(refl_ref, keep, out_ref):
    _, groups, block, window = refl_ref.shape
    wide = 2 * block
    groups = range(groups)
    firsts, seconds, sfirst, ssecond = [], [], [], []
    col = lax.broadcasted_iota(jnp.int32, (block, window), 1)
    for g in groups:
        a = refl_ref[0, g]
        b = jnp.where(keep | (col < block), refl_ref[1, g], 0.0)
        firsts.append(a)
        seconds.append(b)
        sfirst.append(a * (2.0 / jnp.sum(a * a, 1, keepdims=True)))
        ssecond.append(b * (2.0 / jnp.sum(b * b, 1, keepdims=True)))
    above = lax.broadcasted_iota(jnp.int32, (block, wide), 0) < (
        lax.broadcasted_iota(jnp.int32, (block, wide), 1) % block
    )
    near, cross = [], []
    for g in groups:
        ha = halves(firsts[g])
        gq = mm(ssecond[g], halves(seconds[g]), NT)
        gp = mm(sfirst[g], ha, NT)
        near.append(jnp.where(above, jnp.concatenate([gq, gp], 1), 0.0))
        cross.append(
            mm(ssecond[g][:, :block], (ha[0][:, block:], ha[1][:, block:]), NT)
        )

    def diagonal(value, size):
        mask = same_block((wide, wide), size, size, wide)
        return tuple(
            jnp.where(mask, jnp.concatenate([part] * (wide // size), 0), jnp.zeros((), BF16))
            for part in halves(value)
        )

    def gather_blocks(value, size):
        total = None
        for place in range(block // size):
            part = value[place * size : (place + 1) * size]
            pcol = lax.broadcasted_iota(jnp.int32, part.shape, 1)
            part = jnp.where((pcol % block) // size == place, part, 0.0)
            total = part if total is None else total + part
        return total

    def widen(value, size):
        old = value.shape[0]
        tall = jnp.concatenate([value] * (size // old), 0)
        return jnp.where(same_block(tall.shape, old, old, size), tall, 0.0)

    def quad(result, ring, size):
        across = [mm(r, diagonal(b, size)) for r, b in zip(result, ring)]
        halved = [halves(x) for x in across]
        once = [r - mm(x, diagonal(r, size)) for r, x in zip(result, halved)]
        square = [mm(h, diagonal(x, size)) for h, x in zip(halved, across)]
        return [o + mm(s, diagonal(o, size)) for o, s in zip(once, square)]

    small = [gather_blocks(n, 16) for n in near]
    shape = small[0].shape
    row = lax.broadcasted_iota(jnp.int32, shape, 0)
    scol = lax.broadcasted_iota(jnp.int32, shape, 1)
    eye = jnp.where(row == scol % 16, 1.0, 0.0)
    inner = (row // 4) == (scol % 16) // 4
    tiny = [jnp.where(inner, n, 0.0) for n in small]
    square = [mm(n, diagonal(n, 16)) for n in tiny]
    result = [eye - n for n in tiny]
    result = [r + mm(r, diagonal(s, 16)) for r, s in zip(result, square)]
    result = quad(result, [jnp.where(inner, 0.0, n) for n in small], 16)
    middle = [gather_blocks(n, 64) for n in near]
    mmask = same_block(middle[0].shape, 16, 16, 64)
    result = [widen(r, 64) for r in result]
    result = quad(result, [jnp.where(mmask, 0.0, n) for n in middle], 64)
    result = [widen(r, block) for r in result]
    bmask = same_block((block, wide), 64, 64, block)
    across = [mm(r, diagonal(jnp.where(bmask, 0.0, n), block)) for r, n in zip(result, near)]
    result = [r - mm(x, diagonal(r, block)) for r, x in zip(result, across)]
    for g in groups:
        q, p = halves(result[g][:, :block]), halves(result[g][:, block:])
        link = mm(q, cross[g])
        link = mm(link, p)
        solved_p = mm(p, sfirst[g])
        low = halves(sfirst[g])
        solved_q = mm(q, ssecond[g])
        reach = mm(link, low)
        zero = jnp.zeros((block, block), F32)
        sq = jnp.concatenate([-reach[:, :block], solved_q[:, :block] - reach[:, block:], solved_q[:, block:]], 1)
        sp = jnp.concatenate([solved_p, zero], 1)
        solved = jnp.concatenate([sq, sp], 0)
        joined = jnp.concatenate(
            [
                jnp.concatenate([zero, seconds[g]], 1),
                jnp.concatenate([firsts[g], zero], 1),
            ],
            0,
        )
        moved = mm(joined, solved, TN)
        orow = lax.broadcasted_iota(jnp.int32, moved.shape, 0)
        ocol = lax.broadcasted_iota(jnp.int32, moved.shape, 1)
        out_ref[g] = jnp.where(orow == ocol, 1.0, 0.0) - moved


def pick_near(node, core, value):
    block = value.shape[0] // 3
    send_up = (core == 0) & ((node & 1) == 1)
    return jnp.where(send_up, value[:block], value[2 * block :])


def pick_far(node, value):
    block = value.shape[0] // 3
    return jnp.where((node & 2) == 0, value[2 * block :], value[:block])


def half_of(core, value):
    rows = value.shape[0] // PAIR
    return jnp.where(core == 0, value[:rows], value[rows:])


def assemble(place_ref, mine, theirs, groups, refl_ref):
    core, vec = place_ref[1], place_ref[2]
    rows = mine[0].shape[1]
    for step, (own, other) in enumerate(zip(mine, theirs)):
        at = pl.ds(pl.multiple_of((step ^ vec) * rows, rows), rows)
        for slot, group in enumerate(groups):
            refl_ref[core, slot, at, :] = own[group]
            refl_ref[1 - core, slot, at, :] = other[group]


def first_kernel(count, nodes, place_ref, *refs):
    mine, theirs = refs[:count], refs[count : 2 * count]
    top_ref, low_ref, near_ref, far_ref = refs[2 * count : 2 * count + 4]
    oper_ref, fixed_ref, out_near, out_far, refl_ref = refs[2 * count + 4 :]
    block = top_ref.shape[0]
    node, core = place_ref[0], place_ref[1]
    assemble(place_ref, mine, theirs, [0], refl_ref)
    pair_operators(refl_ref, node != nodes - 1, oper_ref)
    below = jnp.where((node & 1) == 0, near_ref[...], far_ref[...])
    window = jnp.concatenate(
        [
            jnp.where(node == 0, top_ref[...], 0.0),
            low_ref[...],
            jnp.where(node == nodes - 1, 0.0, below),
        ],
        0,
    )
    fixed = mm(oper_ref[0], window)
    fixed_ref[...] = fixed
    lead = oper_ref[0, :, :block]
    out_near[:block] = pick_near(node, core, fixed)
    out_near[block:] = pick_near(node, core, lead)
    out_far[...] = jnp.where(core == 0, pick_far(node, fixed), pick_far(node, lead))


def later_kernel(count, nodes, place_ref, *refs):
    mine, theirs = refs[:count], refs[count : 2 * count]
    oper_ref, map_near, map_far, refl_ref = refs[2 * count :]
    node, core = place_ref[0], place_ref[1]
    later, _, size = oper_ref.shape
    assemble(place_ref, mine, theirs, range(1, 1 + later), refl_ref)
    pair_operators(refl_ref, node != nodes - 1, oper_ref)
    leads = [oper_ref[slot, :, : size // 3] for slot in range(later)]
    map_near[...] = jnp.concatenate([pick_near(node, core, lead) for lead in leads], 0)
    map_far[...] = half_of(core, jnp.concatenate([pick_far(node, lead) for lead in leads], 0))


def next_kernel(group, place_ref, *refs):
    (near_ref, far_ref, near2_ref, far2_ref), refs = refs[:4], refs[4:]
    node, core = place_ref[0], place_ref[1]
    here = core == 0
    odd, high = (node & 1) == 1, (node & 2) == 2
    near, near2, far, far2 = near_ref[...], near2_ref[...], far_ref[...], far2_ref[...]
    came1 = jnp.where(here, near, near2)
    came2 = jnp.where(here, near2, near)
    came3 = jnp.concatenate([jnp.where(here, far, far2), jnp.where(here, far2, far)], 0)
    if group == 0:
        block = came1.shape[0] // 2
        map1, map2, map3 = came1[block:], came2[block:], came3[block:]
        came1, came2, came3 = came1[:block], came2[:block], came3[:block]
    else:
        (mnear_ref, mfar_ref, mnear2_ref, mfar2_ref), refs = refs[:4], refs[4:]
        block = came1.shape[0]
        at = slice((group - 1) * block, group * block)
        map1 = jnp.where(here, mnear_ref[at], mnear2_ref[at])
        map2 = jnp.where(here, mnear2_ref[at], mnear_ref[at])
        mfar, mfar2 = mfar_ref[...], mfar2_ref[...]
        map3 = jnp.concatenate(
            [jnp.where(here, mfar, mfar2), jnp.where(here, mfar2, mfar)], 0
        )[at]
    (fixed_ref, first_ref, later_ref), outs = refs[:3], refs[3:]
    oper = first_ref.at[0] if group == 0 else later_ref.at[group - 1]
    carry = jnp.where(high, jnp.where(odd, came3, came2), came1)
    carry = jnp.where(node == 0, 0.0, carry)
    step = jnp.where(odd, came2, came3) + mm(jnp.where(odd, map2, map3), carry)
    carry = jnp.where(high, step, carry)
    step = came1 + mm(map1, carry)
    carry = jnp.where(node == 3, step, carry)
    if len(outs) == 1:
        at = pl.ds(pl.multiple_of(core * block, block), block)
        outs[0][...] = fixed_ref[at, :] + mm(oper[at, :block], carry)
        return
    fixed, lead = fixed_ref[...], oper[:, :block]
    cols = fixed.shape[1]
    below = mm(
        jnp.where(odd, map3, map1), jnp.concatenate([fixed[2 * block :], lead[2 * block :]], 1)
    )
    offset = jnp.where(odd, came3, came1)
    below = jnp.where(node == 3, 0.0, below + jnp.concatenate([offset, jnp.zeros_like(lead[:block])], 1))
    first = jnp.where(node == 0, fixed[:block], 0.0)
    window = jnp.concatenate(
        [
            jnp.concatenate([first, jnp.zeros_like(lead[:block])], 1),
            jnp.concatenate([fixed[block : 2 * block], lead[block : 2 * block]], 1),
            below,
        ],
        0,
    )
    moved = mm(later_ref[group], window)
    fixed = moved[:, :cols] + mm(moved[:, cols:], carry)
    outs[0][...] = fixed
    outs[1][...] = pick_near(node, core, fixed)
    outs[2][...] = half_of(core, pick_far(node, fixed))


def call(kernel, outs, operands, scratch=(), work=0):
    vmem = pl.BlockSpec(memory_space=pltpu.VMEM)
    return pl.pallas_call(
        kernel,
        out_shape=[jax.ShapeDtypeStruct(shape, F32) for shape in outs],
        in_specs=[pl.BlockSpec(memory_space=pltpu.SMEM)] + [vmem] * (len(operands) - 1),
        out_specs=[vmem] * len(outs),
        scratch_shapes=list(scratch),
        cost_estimate=pl.CostEstimate(flops=work, bytes_accessed=0, transcendentals=0),
        compiler_params=pltpu.CompilerParams(vmem_limit_bytes=16 << 20),
    )(*operands)


def dot(left, right):
    return jnp.matmul(left, right, precision=lax.Precision.HIGHEST)


def spread(value, axis, size):
    if size & (size - 1) or size > 8:
        gathered = lax.all_gather(value, axis)
        return [gathered[place] for place in range(size)], False
    return [value] + [
        lax.ppermute(value, axis, [(place, place ^ mask) for place in range(size)])
        for mask in range(1, size)
    ], True


def many_pairs(fixed, operators, node, nodes, row_count):
    groups, block = len(operators), fixed.shape[0] // 3
    members = [[place * PAIR + core for place in range(nodes)] for core in range(PAIR)]
    for group in range(groups):
        lead = operators[group][:, :block]
        down = jnp.concatenate([fixed[2 * block :], lead[2 * block :]], 0)
        up = jnp.concatenate([fixed[:block], lead[:block]], 0)
        earlier = lax.all_gather(down, "rows", axis_index_groups=members)
        later = lax.ppermute(
            up, "rows", [(place, place - PAIR) for place in range(PAIR, row_count)]
        )
        carry = jnp.zeros((block, fixed.shape[1]), F32)
        for place in range(nodes - 1):
            step = earlier[place, :block] + dot(earlier[place, block:], carry)
            carry = jnp.where(node > place, step, carry)
        result = fixed + dot(lead, carry)
        if group < groups - 1:
            below = later[:block] + dot(later[block:], result[2 * block :])
            window = jnp.concatenate(
                [
                    jnp.where(node == 0, result[:block], 0.0),
                    result[block : 2 * block],
                    jnp.where(node == nodes - 1, 0.0, below),
                ],
                0,
            )
            fixed = dot(operators[group + 1], window)
    return result


def local(vectors, reflectors):
    groups, _, _, window = reflectors.shape
    block = window // 2
    cols = vectors.shape[1]
    row_index = lax.axis_index("rows")
    row_count = lax.axis_size("rows")
    vec_index = lax.axis_index("vecs")
    vec_count = lax.axis_size("vecs")
    nodes = row_count // PAIR
    node = row_index // PAIR
    core = row_index % PAIR

    def swap(value, masks):
        moves = [
            (place, ((place // PAIR) ^ masks[place % PAIR]) * PAIR + place % PAIR)
            for place in range(row_count)
        ]
        return lax.ppermute(value, "rows", moves)

    def across(value):
        return lax.ppermute(value, "rows", [(place, place ^ 1) for place in range(row_count)])

    mine, mixed = spread(reflectors[:, 0], "vecs", vec_count)
    other = across(vectors)
    top = jnp.where(core == 0, vectors, other)
    low = jnp.where(core == 0, other, vectors)
    if nodes == 4:
        below = [swap(top, (1, 1)), swap(top, (3, 3))]
    else:
        below = [
            lax.ppermute(
                top, "rows", [(place, place - PAIR) for place in range(PAIR, row_count)]
            )
        ] * 2
    theirs = [across(piece) for piece in mine]
    mine[0] = jnp.where(vec_index < 0, 0.0, mine[0])
    place = jnp.stack([node, core, vec_index if mixed else 0]).astype(jnp.int32)
    later = groups - 1
    work = 16 * (3 * block) ** 3
    pieces = [place, *mine, *theirs]
    first_oper, fixed, near, far = call(
        functools.partial(first_kernel, len(mine), nodes),
        [
            (1, 3 * block, 3 * block),
            (3 * block, cols),
            (2 * block, cols),
            (block, cols),
        ],
        [*pieces, top, low, *below],
        [pltpu.VMEM((PAIR, 1, block, window), F32)],
        work,
    )
    later_oper, *maps = call(
        functools.partial(later_kernel, len(mine), nodes),
        [
            (later, 3 * block, 3 * block),
            (later * block, block),
            (later * block // PAIR, block),
        ],
        pieces,
        [pltpu.VMEM((PAIR, later, block, window), F32)],
        work * later,
    )
    if nodes != 4:
        operators = [first_oper[0]] + [later_oper[slot] for slot in range(later)]
        result = many_pairs(fixed, operators, node, nodes, row_count)
        return jnp.where(core == 0, result[:block], result[block : 2 * block])
    hold = lax.optimization_barrier
    for group in range(groups):
        near = swap(near, (1, 2))
        far = swap(far, (3, 3))
        if group == 0:
            near, *maps = hold((near, *maps))
            maps = [swap(maps[0], (1, 2)), swap(maps[1], (3, 3))]
        elif group == 1:
            far, *maps = hold((far, *maps))
            maps += [across(part) for part in maps]
        came = [near, far, across(near), across(far)]
        operands = [place, *came, *(maps if group else []), fixed, first_oper, later_oper]
        if group < groups - 1:
            fixed, near, far = call(
                functools.partial(next_kernel, group),
                [(3 * block, cols), (block, cols), (block // PAIR, cols)],
                operands,
            )
        else:
            (result,) = call(
                functools.partial(next_kernel, group), [(block, cols)], operands
            )
    return result


def solution(mesh):
    placed = (P("rows", "vecs"), P(None, "rows", "vecs", None))
    return jax.shard_map(
        local, mesh=mesh, in_specs=placed, out_specs=P("rows", "vecs"), check_vma=False
    )
```

```python
import functools
import jax
import jax.numpy as jnp
from jax import lax
from jax.experimental import pallas as pl
from jax.experimental.pallas import tpu as pltpu
from jax.sharding import PartitionSpec as P

PAIR = 2
F32, BF16 = jnp.float32, jnp.bfloat16
NN = ((1,), (0,))
NT = ((1,), (1,))
TN = ((0,), (0,))


def halves(value):
    high = value.astype(BF16)
    return high, (value - high.astype(F32)).astype(BF16)


def mm(left, right, dims=NN):
    left = left if isinstance(left, tuple) else halves(left)
    right = right if isinstance(right, tuple) else halves(right)

    (lc,), (rc,) = dims
    return lax.dot_general(
        jnp.concatenate([left[0], left[0], left[1]], lc),
        jnp.concatenate([right[0], right[1], right[0]], rc),
        (dims, ((), ())),
        preferred_element_type=F32,
    )


def same_block(shape, rows_block, cols_block, wrap):
    row = lax.broadcasted_iota(jnp.int32, shape, 0)
    col = lax.broadcasted_iota(jnp.int32, shape, 1)
    return (row // rows_block) == ((col % wrap) // cols_block)


def pair_operators(refl_ref, keep, out_ref):
    _, groups, block, window = refl_ref.shape
    wide = 2 * block
    groups = range(groups)
    firsts, seconds, sfirst, ssecond = [], [], [], []
    col = lax.broadcasted_iota(jnp.int32, (block, window), 1)
    for g in groups:
        a = refl_ref[0, g]
        b = jnp.where(keep | (col < block), refl_ref[1, g], 0.0)
        firsts.append(a)
        seconds.append(b)
        sfirst.append(a * (2.0 / jnp.sum(a * a, 1, keepdims=True)))
        ssecond.append(b * (2.0 / jnp.sum(b * b, 1, keepdims=True)))
    above = lax.broadcasted_iota(jnp.int32, (block, wide), 0) < (
        lax.broadcasted_iota(jnp.int32, (block, wide), 1) % block
    )
    near, cross = [], []
    for g in groups:
        ha = halves(firsts[g])
        gq = mm(ssecond[g], halves(seconds[g]), NT)
        gp = mm(sfirst[g], ha, NT)
        near.append(jnp.where(above, jnp.concatenate([gq, gp], 1), 0.0))
        cross.append(
            mm(ssecond[g][:, :block], (ha[0][:, block:], ha[1][:, block:]), NT)
        )

    def diagonal(value, size):
        mask = same_block((wide, wide), size, size, wide)
        return tuple(
            jnp.where(mask, jnp.concatenate([part] * (wide // size), 0), jnp.zeros((), BF16))
            for part in halves(value)
        )

    def gather_blocks(value, size):
        total = None
        for place in range(block // size):
            part = value[place * size : (place + 1) * size]
            pcol = lax.broadcasted_iota(jnp.int32, part.shape, 1)
            part = jnp.where((pcol % block) // size == place, part, 0.0)
            total = part if total is None else total + part
        return total

    def widen(value, size):
        old = value.shape[0]
        tall = jnp.concatenate([value] * (size // old), 0)
        return jnp.where(same_block(tall.shape, old, old, size), tall, 0.0)

    def quad(result, ring, size):
        across = [mm(r, diagonal(b, size)) for r, b in zip(result, ring)]
        halved = [halves(x) for x in across]
        once = [r - mm(x, diagonal(r, size)) for r, x in zip(result, halved)]
        square = [mm(h, diagonal(x, size)) for h, x in zip(halved, across)]
        return [o + mm(s, diagonal(o, size)) for o, s in zip(once, square)]

    small = [gather_blocks(n, 16) for n in near]
    shape = small[0].shape
    row = lax.broadcasted_iota(jnp.int32, shape, 0)
    scol = lax.broadcasted_iota(jnp.int32, shape, 1)
    eye = jnp.where(row == scol % 16, 1.0, 0.0)
    inner = (row // 4) == (scol % 16) // 4
    tiny = [jnp.where(inner, n, 0.0) for n in small]
    square = [mm(n, diagonal(n, 16)) for n in tiny]
    result = [eye - n for n in tiny]
    result = [r + mm(r, diagonal(s, 16)) for r, s in zip(result, square)]
    result = quad(result, [jnp.where(inner, 0.0, n) for n in small], 16)
    middle = [gather_blocks(n, 64) for n in near]
    mmask = same_block(middle[0].shape, 16, 16, 64)
    result = [widen(r, 64) for r in result]
    result = quad(result, [jnp.where(mmask, 0.0, n) for n in middle], 64)
    result = [widen(r, block) for r in result]
    bmask = same_block((block, wide), 64, 64, block)
    across = [mm(r, diagonal(jnp.where(bmask, 0.0, n), block)) for r, n in zip(result, near)]
    result = [r - mm(x, diagonal(r, block)) for r, x in zip(result, across)]
    for g in groups:
        q, p = halves(result[g][:, :block]), halves(result[g][:, block:])
        link = mm(q, cross[g])
        link = mm(link, p)
        solved_p = mm(p, sfirst[g])
        low = halves(sfirst[g])
        solved_q = mm(q, ssecond[g])
        reach = mm(link, low)
        zero = jnp.zeros((block, block), F32)
        sq = jnp.concatenate([-reach[:, :block], solved_q[:, :block] - reach[:, block:], solved_q[:, block:]], 1)
        sp = jnp.concatenate([solved_p, zero], 1)
        solved = jnp.concatenate([sq, sp], 0)
        joined = jnp.concatenate(
            [
                jnp.concatenate([zero, seconds[g]], 1),
                jnp.concatenate([firsts[g], zero], 1),
            ],
            0,
        )
        moved = mm(joined, solved, TN)
        orow = lax.broadcasted_iota(jnp.int32, moved.shape, 0)
        ocol = lax.broadcasted_iota(jnp.int32, moved.shape, 1)
        out_ref[g] = jnp.where(orow == ocol, 1.0, 0.0) - moved


def pick_near(node, core, value):
    block = value.shape[0] // 3
    send_up = (core == 0) & ((node & 1) == 1)
    return jnp.where(send_up, value[:block], value[2 * block :])


def pick_far(node, value):
    block = value.shape[0] // 3
    return jnp.where((node & 2) == 0, value[2 * block :], value[:block])


def half_of(core, value):
    rows = value.shape[0] // PAIR
    return jnp.where(core == 0, value[:rows], value[rows:])


def assemble(place_ref, mine, theirs, skip, refl_ref):
    core, vec = place_ref[1], place_ref[2]
    count, rows = refl_ref.shape[1], mine[0].shape[1]
    for step, (own, other) in enumerate(zip(mine, theirs)):
        at = pl.ds(pl.multiple_of((step ^ vec) * rows, rows), rows)
        first = min(skip, own.shape[0] - count)
        for slot in range(count):
            refl_ref[core, slot, at, :] = own[first + slot]
            refl_ref[1 - core, slot, at, :] = other[first + slot]


def first_kernel(count, nodes, place_ref, *refs):
    mine, theirs = refs[:count], refs[count : 2 * count]
    top_ref, low_ref, near_ref, far_ref = refs[2 * count : 2 * count + 4]
    oper_ref, fixed_ref, out_near, out_far, refl_ref = refs[2 * count + 4 :]
    block = top_ref.shape[0]
    node, core = place_ref[0], place_ref[1]
    assemble(place_ref, mine, theirs, 0, refl_ref)
    pair_operators(refl_ref, node != nodes - 1, oper_ref)
    below = jnp.where((node & 1) == 0, near_ref[...], far_ref[...])
    window = jnp.concatenate(
        [
            jnp.where(node == 0, top_ref[...], 0.0),
            low_ref[...],
            jnp.where(node == nodes - 1, 0.0, below),
        ],
        0,
    )
    fixed = mm(oper_ref[0], window)
    fixed_ref[...] = fixed
    lead = oper_ref[0, :, :block]
    out_near[:block] = pick_near(node, core, fixed)
    out_near[block:] = pick_near(node, core, lead)
    out_far[...] = jnp.where(core == 0, pick_far(node, fixed), pick_far(node, lead))


def later_kernel(count, nodes, place_ref, *refs):
    mine, theirs = refs[:count], refs[count : 2 * count]
    oper_ref, map_near, map_far, refl_ref = refs[2 * count :]
    node, core = place_ref[0], place_ref[1]
    later, _, size = oper_ref.shape
    assemble(place_ref, mine, theirs, 1, refl_ref)
    pair_operators(refl_ref, node != nodes - 1, oper_ref)
    leads = [oper_ref[slot, :, : size // 3] for slot in range(later)]
    map_near[...] = jnp.concatenate([pick_near(node, core, lead) for lead in leads], 0)
    map_far[...] = half_of(core, jnp.concatenate([pick_far(node, lead) for lead in leads], 0))


def next_kernel(group, place_ref, *refs):
    (near_ref, far_ref, near2_ref, far2_ref), refs = refs[:4], refs[4:]
    node, core = place_ref[0], place_ref[1]
    here = core == 0
    odd, high = (node & 1) == 1, (node & 2) == 2
    near, near2, far, far2 = near_ref[...], near2_ref[...], far_ref[...], far2_ref[...]
    came1 = jnp.where(here, near, near2)
    came2 = jnp.where(here, near2, near)
    came3 = jnp.concatenate([jnp.where(here, far, far2), jnp.where(here, far2, far)], 0)
    if group == 0:
        block = came1.shape[0] // 2
        map1, map2, map3 = came1[block:], came2[block:], came3[block:]
        came1, came2, came3 = came1[:block], came2[:block], came3[:block]
    else:
        (mnear_ref, mfar_ref, mnear2_ref, mfar2_ref), refs = refs[:4], refs[4:]
        block = came1.shape[0]
        at = slice((group - 1) * block, group * block)
        map1 = jnp.where(here, mnear_ref[at], mnear2_ref[at])
        map2 = jnp.where(here, mnear2_ref[at], mnear_ref[at])
        mfar, mfar2 = mfar_ref[...], mfar2_ref[...]
        map3 = jnp.concatenate(
            [jnp.where(here, mfar, mfar2), jnp.where(here, mfar2, mfar)], 0
        )[at]
    (fixed_ref, first_ref, later_ref), outs = refs[:3], refs[3:]
    oper = first_ref.at[0] if group == 0 else later_ref.at[group - 1]
    carry = jnp.where(high, jnp.where(odd, came3, came2), came1)
    carry = jnp.where(node == 0, 0.0, carry)
    step = jnp.where(odd, came2, came3) + mm(jnp.where(odd, map2, map3), carry)
    carry = jnp.where(high, step, carry)
    step = came1 + mm(map1, carry)
    carry = jnp.where(node == 3, step, carry)
    if len(outs) == 1:
        at = pl.ds(pl.multiple_of(core * block, block), block)
        outs[0][...] = fixed_ref[at, :] + mm(oper[at, :block], carry)
        return
    fixed, lead = fixed_ref[...], oper[:, :block]
    cols = fixed.shape[1]
    below = mm(
        jnp.where(odd, map3, map1), jnp.concatenate([fixed[2 * block :], lead[2 * block :]], 1)
    )
    offset = jnp.where(odd, came3, came1)
    below = jnp.where(node == 3, 0.0, below + jnp.concatenate([offset, jnp.zeros_like(lead[:block])], 1))
    first = jnp.where(node == 0, fixed[:block], 0.0)
    window = jnp.concatenate(
        [
            jnp.concatenate([first, jnp.zeros_like(lead[:block])], 1),
            jnp.concatenate([fixed[block : 2 * block], lead[block : 2 * block]], 1),
            below,
        ],
        0,
    )
    moved = mm(later_ref[group], window)
    fixed = moved[:, :cols] + mm(moved[:, cols:], carry)
    outs[0][...] = fixed
    outs[1][...] = pick_near(node, core, fixed)
    outs[2][...] = half_of(core, pick_far(node, fixed))


def call(kernel, outs, operands, scratch=(), work=0):
    vmem = pl.BlockSpec(memory_space=pltpu.VMEM)
    return pl.pallas_call(
        kernel,
        out_shape=[jax.ShapeDtypeStruct(shape, F32) for shape in outs],
        in_specs=[pl.BlockSpec(memory_space=pltpu.SMEM)] + [vmem] * (len(operands) - 1),
        out_specs=[vmem] * len(outs),
        scratch_shapes=list(scratch),
        cost_estimate=pl.CostEstimate(flops=work, bytes_accessed=0, transcendentals=0),
        compiler_params=pltpu.CompilerParams(vmem_limit_bytes=16 << 20),
    )(*operands)


def dot(left, right):
    return jnp.matmul(left, right, precision=lax.Precision.HIGHEST)


def many_pairs(fixed, operators, node, nodes, row_count):
    groups, block = len(operators), fixed.shape[0] // 3
    members = [[place * PAIR + core for place in range(nodes)] for core in range(PAIR)]
    for group in range(groups):
        lead = operators[group][:, :block]
        down = jnp.concatenate([fixed[2 * block :], lead[2 * block :]], 0)
        up = jnp.concatenate([fixed[:block], lead[:block]], 0)
        earlier = lax.all_gather(down, "rows", axis_index_groups=members)
        later = lax.ppermute(
            up, "rows", [(place, place - PAIR) for place in range(PAIR, row_count)]
        )
        carry = jnp.zeros((block, fixed.shape[1]), F32)
        for place in range(nodes - 1):
            step = earlier[place, :block] + dot(earlier[place, block:], carry)
            carry = jnp.where(node > place, step, carry)
        result = fixed + dot(lead, carry)
        if group < groups - 1:
            below = later[:block] + dot(later[block:], result[2 * block :])
            window = jnp.concatenate(
                [
                    jnp.where(node == 0, result[:block], 0.0),
                    result[block : 2 * block],
                    jnp.where(node == nodes - 1, 0.0, below),
                ],
                0,
            )
            fixed = dot(operators[group + 1], window)
    return result


def local(vectors, reflectors):
    groups, _, _, window = reflectors.shape
    block = window // 2
    cols = vectors.shape[1]
    row_index = lax.axis_index("rows")
    row_count = lax.axis_size("rows")
    vec_index = lax.axis_index("vecs")
    vec_count = lax.axis_size("vecs")
    nodes = row_count // PAIR
    node = row_index // PAIR
    core = row_index % PAIR

    def swap(value, masks):
        moves = [
            (place, ((place // PAIR) ^ masks[place % PAIR]) * PAIR + place % PAIR)
            for place in range(row_count)
        ]
        return lax.ppermute(value, "rows", moves)

    def across(value):
        return lax.ppermute(value, "rows", [(place, place ^ 1) for place in range(row_count)])

    hold = lax.optimization_barrier
    later = groups - 1
    blocks = reflectors[:, 0]
    other = across(vectors)
    if vec_count & (vec_count - 1) or vec_count > 8:
        gathered = lax.all_gather(blocks, "vecs")
        mine = rest = [gathered[step] for step in range(vec_count)]
        start = 0
    else:

        def partners(value, mask):
            return lax.ppermute(
                value, "vecs", [(step, step ^ mask) for step in range(vec_count)]
            )

        mine = [blocks, partners(blocks, 1)]
        mine += [partners(blocks[:1], mask) for mask in range(vec_count - 1, 1, -1)]
        behind, other = hold((blocks[1:], other))
        rest = mine[:2] + [partners(behind, mask) for mask in range(vec_count - 1, 1, -1)]
        order = [0, 1] + list(range(vec_count - 1, 1, -1))
        mine, rest = ([part[order.index(step)] for step in range(vec_count)] for part in (mine, rest))
        start = vec_index
    top = jnp.where(core == 0, vectors, other)
    low = jnp.where(core == 0, other, vectors)
    if nodes == 4:
        below = [swap(top, (1, 1)), swap(top, (3, 3))]
    else:
        below = [
            lax.ppermute(
                top, "rows", [(place, place - PAIR) for place in range(PAIR, row_count)]
            )
        ] * 2
    theirs = [across(piece) for piece in mine]
    whole = jnp.where(vec_index < 0, 0.0, blocks)
    place = jnp.stack([node, core, start]).astype(jnp.int32)
    work = 16 * (3 * block) ** 3
    first_oper, fixed, near, far = call(
        functools.partial(first_kernel, vec_count, nodes),
        [
            (1, 3 * block, 3 * block),
            (3 * block, cols),
            (2 * block, cols),
            (block, cols),
        ],
        [place, *([whole] + mine[1:]), *theirs, top, low, *below],
        [pltpu.VMEM((PAIR, 1, block, window), F32)],
        0,
    )
    far, *rest[2:] = hold((far, *rest[2:]))
    theirs = theirs[:2] + [across(piece) for piece in rest[2:]]
    later_oper, *maps = call(
        functools.partial(later_kernel, vec_count, nodes),
        [
            (later, 3 * block, 3 * block),
            (later * block, block),
            (later * block // PAIR, block),
        ],
        [place, *([whole] + rest[1:]), *theirs],
        [pltpu.VMEM((PAIR, later, block, window), F32)],
        work * later,
    )
    if nodes != 4:
        operators = [first_oper[0]] + [later_oper[slot] for slot in range(later)]
        result = many_pairs(fixed, operators, node, nodes, row_count)
        return jnp.where(core == 0, result[:block], result[block : 2 * block])
    for group in range(groups):
        near = swap(near, (1, 2))
        far = swap(far, (3, 3))
        if group == 0:
            near, *maps = hold((near, *maps))
            maps = [swap(maps[0], (1, 2)), swap(maps[1], (3, 3))]
        elif group == 1:
            far, *maps = hold((far, *maps))
            maps += [across(part) for part in maps]
        came = [near, far, across(near), across(far)]
        operands = [place, *came, *(maps if group else []), fixed, first_oper, later_oper]
        if group < groups - 1:
            fixed, near, far = call(
                functools.partial(next_kernel, group),
                [(3 * block, cols), (block, cols), (block // PAIR, cols)],
                operands,
            )
        else:
            (result,) = call(
                functools.partial(next_kernel, group), [(block, cols)], operands
            )
    return result


def solution(mesh):
    placed = (P("rows", "vecs"), P(None, "rows", "vecs", None))
    return jax.shard_map(
        local, mesh=mesh, in_specs=placed, out_specs=P("rows", "vecs"), check_vma=False
    )
```

```python
import functools
import jax
import jax.numpy as jnp
from jax import lax
from jax.experimental import pallas as pl
from jax.experimental.pallas import tpu as pltpu
from jax.sharding import PartitionSpec as P

PAIR = 2
F32, BF16 = jnp.float32, jnp.bfloat16
NN = ((1,), (0,))
NT = ((1,), (1,))
TN = ((0,), (0,))


def halves(value):
    high = value.astype(BF16)
    return high, (value - high.astype(F32)).astype(BF16)


def mm(left, right, dims=NN):
    left = left if isinstance(left, tuple) else halves(left)
    right = right if isinstance(right, tuple) else halves(right)

    (lc,), (rc,) = dims
    return lax.dot_general(
        jnp.concatenate([left[0], left[0], left[1]], lc),
        jnp.concatenate([right[0], right[1], right[0]], rc),
        (dims, ((), ())),
        preferred_element_type=F32,
    )


def same_block(shape, rows_block, cols_block, wrap):
    row = lax.broadcasted_iota(jnp.int32, shape, 0)
    col = lax.broadcasted_iota(jnp.int32, shape, 1)
    return (row // rows_block) == ((col % wrap) // cols_block)


def pair_operators(refl_ref, keep, out_ref):
    _, groups, block, window = refl_ref.shape
    wide = 2 * block
    groups = range(groups)
    firsts, seconds, sfirst, ssecond = [], [], [], []
    col = lax.broadcasted_iota(jnp.int32, (block, window), 1)
    for g in groups:
        a = refl_ref[0, g]
        b = jnp.where(keep | (col < block), refl_ref[1, g], 0.0)
        firsts.append(a)
        seconds.append(b)
        sfirst.append(a * (2.0 / jnp.sum(a * a, 1, keepdims=True)))
        ssecond.append(b * (2.0 / jnp.sum(b * b, 1, keepdims=True)))
    above = lax.broadcasted_iota(jnp.int32, (block, wide), 0) < (
        lax.broadcasted_iota(jnp.int32, (block, wide), 1) % block
    )
    near, cross = [], []
    for g in groups:
        ha = halves(firsts[g])
        gq = mm(ssecond[g], halves(seconds[g]), NT)
        gp = mm(sfirst[g], ha, NT)
        near.append(jnp.where(above, jnp.concatenate([gq, gp], 1), 0.0))
        cross.append(
            mm(ssecond[g][:, :block], (ha[0][:, block:], ha[1][:, block:]), NT)
        )

    def diagonal(value, size):
        mask = same_block((wide, wide), size, size, wide)
        return tuple(
            jnp.where(mask, jnp.concatenate([part] * (wide // size), 0), jnp.zeros((), BF16))
            for part in halves(value)
        )

    def gather_blocks(value, size):
        total = None
        for place in range(block // size):
            part = value[place * size : (place + 1) * size]
            pcol = lax.broadcasted_iota(jnp.int32, part.shape, 1)
            part = jnp.where((pcol % block) // size == place, part, 0.0)
            total = part if total is None else total + part
        return total

    def widen(value, size):
        old = value.shape[0]
        tall = jnp.concatenate([value] * (size // old), 0)
        return jnp.where(same_block(tall.shape, old, old, size), tall, 0.0)

    def quad(result, ring, size):
        across = [mm(r, diagonal(b, size)) for r, b in zip(result, ring)]
        halved = [halves(x) for x in across]
        once = [r - mm(x, diagonal(r, size)) for r, x in zip(result, halved)]
        square = [mm(h, diagonal(x, size)) for h, x in zip(halved, across)]
        return [o + mm(s, diagonal(o, size)) for o, s in zip(once, square)]

    small = [gather_blocks(n, 16) for n in near]
    shape = small[0].shape
    row = lax.broadcasted_iota(jnp.int32, shape, 0)
    scol = lax.broadcasted_iota(jnp.int32, shape, 1)
    eye = jnp.where(row == scol % 16, 1.0, 0.0)
    inner = (row // 4) == (scol % 16) // 4
    tiny = [jnp.where(inner, n, 0.0) for n in small]
    square = [mm(n, diagonal(n, 16)) for n in tiny]
    result = [eye - n for n in tiny]
    result = [r + mm(r, diagonal(s, 16)) for r, s in zip(result, square)]
    result = quad(result, [jnp.where(inner, 0.0, n) for n in small], 16)
    middle = [gather_blocks(n, 64) for n in near]
    mmask = same_block(middle[0].shape, 16, 16, 64)
    result = [widen(r, 64) for r in result]
    result = quad(result, [jnp.where(mmask, 0.0, n) for n in middle], 64)
    result = [widen(r, block) for r in result]
    bmask = same_block((block, wide), 64, 64, block)
    across = [mm(r, diagonal(jnp.where(bmask, 0.0, n), block)) for r, n in zip(result, near)]
    result = [r - mm(x, diagonal(r, block)) for r, x in zip(result, across)]
    for g in groups:
        q, p = halves(result[g][:, :block]), halves(result[g][:, block:])
        link = mm(q, cross[g])
        link = mm(link, p)
        solved_p = mm(p, sfirst[g])
        low = halves(sfirst[g])
        solved_q = mm(q, ssecond[g])
        reach = mm(link, low)
        zero = jnp.zeros((block, block), F32)
        sq = jnp.concatenate([-reach[:, :block], solved_q[:, :block] - reach[:, block:], solved_q[:, block:]], 1)
        sp = jnp.concatenate([solved_p, zero], 1)
        solved = jnp.concatenate([sq, sp], 0)
        joined = jnp.concatenate(
            [
                jnp.concatenate([zero, seconds[g]], 1),
                jnp.concatenate([firsts[g], zero], 1),
            ],
            0,
        )
        moved = mm(joined, solved, TN)
        orow = lax.broadcasted_iota(jnp.int32, moved.shape, 0)
        ocol = lax.broadcasted_iota(jnp.int32, moved.shape, 1)
        out_ref[g] = jnp.where(orow == ocol, 1.0, 0.0) - moved


def pick_near(node, core, value):
    block = value.shape[0] // 3
    send_up = (core == 0) & ((node & 1) == 1)
    return jnp.where(send_up, value[:block], value[2 * block :])


def pick_far(node, value):
    block = value.shape[0] // 3
    return jnp.where((node & 2) == 0, value[2 * block :], value[:block])


def half_of(core, value):
    rows = value.shape[0] // PAIR
    return jnp.where(core == 0, value[:rows], value[rows:])


def first_kernel(count, nodes, place_ref, *refs):
    mine, theirs = refs[:count], refs[count : 2 * count]
    top_ref, low_ref, near_ref, far_ref = refs[2 * count : 2 * count + 4]
    oper_ref, fixed_ref, out_near, out_far, refl_ref = refs[2 * count + 4 :]
    block = top_ref.shape[0]
    node, core, vec = place_ref[0], place_ref[1], place_ref[2]
    groups, rows, _ = mine[0].shape
    for step in range(count):
        at = pl.ds(pl.multiple_of((step ^ vec) * rows, rows), rows)
        for group in range(groups):
            refl_ref[core, group, at, :] = mine[step][group]
            refl_ref[1 - core, group, at, :] = theirs[step][group]
    pair_operators(refl_ref, node != nodes - 1, oper_ref)
    below = jnp.where((node & 1) == 0, near_ref[...], far_ref[...])
    window = jnp.concatenate(
        [
            jnp.where(node == 0, top_ref[...], 0.0),
            low_ref[...],
            jnp.where(node == nodes - 1, 0.0, below),
        ],
        0,
    )
    fixed = mm(oper_ref[0], window)
    fixed_ref[...] = fixed
    lead = oper_ref[0, :, :block]
    out_near[:block] = pick_near(node, core, fixed)
    out_near[block:] = pick_near(node, core, lead)
    out_far[...] = jnp.where(core == 0, pick_far(node, fixed), pick_far(node, lead))


def between_kernel(group, place_ref, fixed_ref, oper_ref, base_ref, low_ref, *maps):
    node, core = place_ref[0], place_ref[1]
    groups, size, _ = oper_ref.shape
    block = size // 3
    own = slice(block, 2 * block)
    first = jnp.where(node == 0, fixed_ref[:block], 0.0)
    base_ref[...] = mm(
        oper_ref[group + 1, :, : 2 * block], jnp.concatenate([first, fixed_ref[own]], 0)
    )
    low_ref[...] = mm(oper_ref[group + 1, :, own], oper_ref[group, own, :block])
    if maps:
        leads = [oper_ref[later, :, :block] for later in range(1, groups)]
        maps[0][...] = jnp.concatenate([pick_near(node, core, lead) for lead in leads], 0)
        maps[1][...] = half_of(
            core, jnp.concatenate([pick_far(node, lead) for lead in leads], 0)
        )


def next_kernel(group, place_ref, *refs):
    (near_ref, far_ref, near2_ref, far2_ref), refs = refs[:4], refs[4:]
    node, core = place_ref[0], place_ref[1]
    here = core == 0
    odd, high = (node & 1) == 1, (node & 2) == 2
    near, near2, far, far2 = near_ref[...], near2_ref[...], far_ref[...], far2_ref[...]
    came1 = jnp.where(here, near, near2)
    came2 = jnp.where(here, near2, near)
    came3 = jnp.concatenate([jnp.where(here, far, far2), jnp.where(here, far2, far)], 0)
    if group == 0:
        block = came1.shape[0] // 2
        map1, map2, map3 = came1[block:], came2[block:], came3[block:]
        came1, came2, came3 = came1[:block], came2[:block], came3[:block]
    else:
        (mnear_ref, mfar_ref, mnear2_ref, mfar2_ref), refs = refs[:4], refs[4:]
        block = came1.shape[0]
        at = slice((group - 1) * block, group * block)
        map1 = jnp.where(here, mnear_ref[at], mnear2_ref[at])
        map2 = jnp.where(here, mnear2_ref[at], mnear_ref[at])
        mfar, mfar2 = mfar_ref[...], mfar2_ref[...]
        map3 = jnp.concatenate(
            [jnp.where(here, mfar, mfar2), jnp.where(here, mfar2, mfar)], 0
        )[at]
    fixed_ref, oper_ref, refs = refs[0], refs[1], refs[2:]
    carry = jnp.where(high, jnp.where(odd, came3, came2), came1)
    carry = jnp.where(node == 0, 0.0, carry)
    step = jnp.where(odd, came2, came3) + mm(jnp.where(odd, map2, map3), carry)
    carry = jnp.where(high, step, carry)
    step = came1 + mm(map1, carry)
    carry = jnp.where(node == 3, step, carry)
    if len(refs) == 1:
        at = pl.ds(pl.multiple_of(core * block, block), block)
        refs[0][...] = fixed_ref[at, :] + mm(oper_ref[group, at, :block], carry)
        return
    base_ref, low_ref, out_fixed, out_near, out_far = refs
    cols = fixed_ref.shape[1]
    out = slice(2 * block, 3 * block)
    reach = mm(
        jnp.where(odd, map3, map1),
        jnp.concatenate([fixed_ref[out], oper_ref[group, out, :block]], 1),
    )
    below = jnp.where(odd, came3, came1) + reach[:, :cols] + mm(reach[:, cols:], carry)
    below = jnp.where(node == 3, 0.0, below)
    fixed = base_ref[...] + mm(
        jnp.concatenate([oper_ref[group + 1, :, out], low_ref[...]], 1),
        jnp.concatenate([below, carry], 0),
    )
    out_fixed[...] = fixed
    out_near[...] = pick_near(node, core, fixed)
    out_far[...] = half_of(core, pick_far(node, fixed))


def call(kernel, outs, operands, scratch=(), work=0):
    vmem = pl.BlockSpec(memory_space=pltpu.VMEM)
    return pl.pallas_call(
        kernel,
        out_shape=[jax.ShapeDtypeStruct(shape, F32) for shape in outs],
        in_specs=[pl.BlockSpec(memory_space=pltpu.SMEM)] + [vmem] * (len(operands) - 1),
        out_specs=[vmem] * len(outs),
        scratch_shapes=list(scratch),
        cost_estimate=pl.CostEstimate(flops=work, bytes_accessed=0, transcendentals=0),
        compiler_params=pltpu.CompilerParams(vmem_limit_bytes=16 << 20),
    )(*operands)


def dot(left, right):
    return jnp.matmul(left, right, precision=lax.Precision.HIGHEST)


def spread(value, axis, size):
    if size & (size - 1) or size > 8:
        gathered = lax.all_gather(value, axis)
        return [gathered[place] for place in range(size)], False
    return [value] + [
        lax.ppermute(value, axis, [(place, place ^ mask) for place in range(size)])
        for mask in range(1, size)
    ], True


def many_pairs(fixed, operators, node, nodes, row_count):
    groups, block = operators.shape[0], fixed.shape[0] // 3
    members = [[place * PAIR + core for place in range(nodes)] for core in range(PAIR)]
    for group in range(groups):
        lead = operators[group][:, :block]
        down = jnp.concatenate([fixed[2 * block :], lead[2 * block :]], 0)
        up = jnp.concatenate([fixed[:block], lead[:block]], 0)
        earlier = lax.all_gather(down, "rows", axis_index_groups=members)
        later = lax.ppermute(
            up, "rows", [(place, place - PAIR) for place in range(PAIR, row_count)]
        )
        carry = jnp.zeros((block, fixed.shape[1]), F32)
        for place in range(nodes - 1):
            step = earlier[place, :block] + dot(earlier[place, block:], carry)
            carry = jnp.where(node > place, step, carry)
        result = fixed + dot(lead, carry)
        if group < groups - 1:
            below = later[:block] + dot(later[block:], result[2 * block :])
            window = jnp.concatenate(
                [
                    jnp.where(node == 0, result[:block], 0.0),
                    result[block : 2 * block],
                    jnp.where(node == nodes - 1, 0.0, below),
                ],
                0,
            )
            fixed = dot(operators[group + 1], window)
    return result


def local(vectors, reflectors):
    groups, _, _, window = reflectors.shape
    block = window // 2
    cols = vectors.shape[1]
    row_index = lax.axis_index("rows")
    row_count = lax.axis_size("rows")
    vec_index = lax.axis_index("vecs")
    vec_count = lax.axis_size("vecs")
    nodes = row_count // PAIR
    node = row_index // PAIR
    core = row_index % PAIR

    def swap(value, masks):
        moves = [
            (place, ((place // PAIR) ^ masks[place % PAIR]) * PAIR + place % PAIR)
            for place in range(row_count)
        ]
        return lax.ppermute(value, "rows", moves)

    def across(value):
        return lax.ppermute(value, "rows", [(place, place ^ 1) for place in range(row_count)])

    mine, mixed = spread(reflectors[:, 0], "vecs", vec_count)
    other = across(vectors)
    top = jnp.where(core == 0, vectors, other)
    low = jnp.where(core == 0, other, vectors)
    if nodes == 4:
        below = [swap(top, (1, 1)), swap(top, (3, 3))]
    else:
        below = [
            lax.ppermute(
                top, "rows", [(place, place - PAIR) for place in range(PAIR, row_count)]
            )
        ] * 2
    theirs = [across(piece) for piece in mine]
    mine[0] = jnp.where(vec_index < 0, 0.0, mine[0])
    place = jnp.stack([node, core, vec_index if mixed else 0]).astype(jnp.int32)
    later = (groups - 1) * block
    size = 3 * block
    operators, fixed, near, far = call(
        functools.partial(first_kernel, len(mine), nodes),
        [(groups, size, size), (size, cols), (2 * block, cols), (block, cols)],
        [place, *mine, *theirs, top, low, *below],
        [pltpu.VMEM((PAIR, groups, block, window), F32)],
    )
    if nodes != 4:
        result = many_pairs(fixed, operators, node, nodes, row_count)
        return jnp.where(core == 0, result[:block], result[block : 2 * block])
    hold = lax.optimization_barrier
    maps = []
    for group in range(groups):
        last_group = group == groups - 1
        near = swap(near, (1, 2))
        far = swap(far, (3, 3))
        if not last_group:
            shapes = [(later, block), (later // PAIR, block)] if group == 0 else []
            base, onto, *sent = call(
                functools.partial(between_kernel, group),
                [(size, cols), (size, block), *shapes],
                [place, fixed, operators],
                work=4 * size * size * cols,
            )
        if group == 1:
            far, *maps = hold((far, *maps))
            maps += [across(part) for part in maps]
        operands = [place, near, far, across(near), across(far), *maps, fixed, operators]
        if group == 0:
            maps = [swap(sent[0], (1, 2)), swap(sent[1], (3, 3))]
        if last_group:
            (result,) = call(functools.partial(next_kernel, group), [(block, cols)], operands)
        else:
            fixed, near, far = call(
                functools.partial(next_kernel, group),
                [(size, cols), (block, cols), (block // PAIR, cols)],
                [*operands, base, onto],
            )
    return result


def solution(mesh):
    placed = (P("rows", "vecs"), P(None, "rows", "vecs", None))
    return jax.shard_map(
        local, mesh=mesh, in_specs=placed, out_specs=P("rows", "vecs"), check_vma=False
    )
```

```python
import functools
import jax
import jax.numpy as jnp
from jax import lax
from jax.experimental import pallas as pl
from jax.experimental.pallas import tpu as pltpu
from jax.sharding import PartitionSpec as P

PAIR = 2
F32, BF16 = jnp.float32, jnp.bfloat16
NN = ((1,), (0,))
NT = ((1,), (1,))
TN = ((0,), (0,))


def halves(value):
    high = value.astype(BF16)
    return high, (value - high.astype(F32)).astype(BF16)


def mm(left, right, dims=NN):
    left = left if isinstance(left, tuple) else halves(left)
    right = right if isinstance(right, tuple) else halves(right)

    (lc,), (rc,) = dims
    return lax.dot_general(
        jnp.concatenate([left[0], left[0], left[1]], lc),
        jnp.concatenate([right[0], right[1], right[0]], rc),
        (dims, ((), ())),
        preferred_element_type=F32,
    )


def same_block(shape, rows_block, cols_block, wrap):
    row = lax.broadcasted_iota(jnp.int32, shape, 0)
    col = lax.broadcasted_iota(jnp.int32, shape, 1)
    return (row // rows_block) == ((col % wrap) // cols_block)


def pair_inverses(refl_ref, keep):
    _, groups, block, window = refl_ref.shape
    wide = 2 * block
    groups = range(groups)
    firsts, seconds, sfirst, ssecond = [], [], [], []
    col = lax.broadcasted_iota(jnp.int32, (block, window), 1)
    for g in groups:
        a = refl_ref[0, g]
        b = jnp.where(keep | (col < block), refl_ref[1, g], 0.0)
        firsts.append(a)
        seconds.append(b)
        sfirst.append(a * (2.0 / jnp.sum(a * a, 1, keepdims=True)))
        ssecond.append(b * (2.0 / jnp.sum(b * b, 1, keepdims=True)))
    above = lax.broadcasted_iota(jnp.int32, (block, wide), 0) < (
        lax.broadcasted_iota(jnp.int32, (block, wide), 1) % block
    )
    near, cross = [], []
    for g in groups:
        ha = halves(firsts[g])
        gq = mm(ssecond[g], halves(seconds[g]), NT)
        gp = mm(sfirst[g], ha, NT)
        near.append(jnp.where(above, jnp.concatenate([gq, gp], 1), 0.0))
        cross.append(
            mm(ssecond[g][:, :block], (ha[0][:, block:], ha[1][:, block:]), NT)
        )

    def diagonal(value, size):
        mask = same_block((wide, wide), size, size, wide)
        return tuple(
            jnp.where(mask, jnp.concatenate([part] * (wide // size), 0), jnp.zeros((), BF16))
            for part in halves(value)
        )

    def gather_blocks(value, size):
        total = None
        for place in range(block // size):
            part = value[place * size : (place + 1) * size]
            pcol = lax.broadcasted_iota(jnp.int32, part.shape, 1)
            part = jnp.where((pcol % block) // size == place, part, 0.0)
            total = part if total is None else total + part
        return total

    def widen(value, size):
        old = value.shape[0]
        tall = jnp.concatenate([value] * (size // old), 0)
        return jnp.where(same_block(tall.shape, old, old, size), tall, 0.0)

    def quad(result, ring, size):
        across = [mm(r, diagonal(b, size)) for r, b in zip(result, ring)]
        halved = [halves(x) for x in across]
        once = [r - mm(x, diagonal(r, size)) for r, x in zip(result, halved)]
        square = [mm(h, diagonal(x, size)) for h, x in zip(halved, across)]
        return [o + mm(s, diagonal(o, size)) for o, s in zip(once, square)]

    small = [gather_blocks(n, 16) for n in near]
    shape = small[0].shape
    row = lax.broadcasted_iota(jnp.int32, shape, 0)
    scol = lax.broadcasted_iota(jnp.int32, shape, 1)
    eye = jnp.where(row == scol % 16, 1.0, 0.0)
    inner = (row // 4) == (scol % 16) // 4
    tiny = [jnp.where(inner, n, 0.0) for n in small]
    square = [mm(n, diagonal(n, 16)) for n in tiny]
    result = [eye - n for n in tiny]
    result = [r + mm(r, diagonal(s, 16)) for r, s in zip(result, square)]
    result = quad(result, [jnp.where(inner, 0.0, n) for n in small], 16)
    middle = [gather_blocks(n, 64) for n in near]
    mmask = same_block(middle[0].shape, 16, 16, 64)
    result = [widen(r, 64) for r in result]
    result = quad(result, [jnp.where(mmask, 0.0, n) for n in middle], 64)
    result = [widen(r, block) for r in result]
    bmask = same_block((block, wide), 64, 64, block)
    across = [mm(r, diagonal(jnp.where(bmask, 0.0, n), block)) for r, n in zip(result, near)]
    result = [r - mm(x, diagonal(r, block)) for r, x in zip(result, across)]
    return [
        (
            firsts[g],
            seconds[g],
            sfirst[g],
            ssecond[g],
            cross[g],
            halves(result[g][:, :block]),
            halves(result[g][:, block:]),
        )
        for g in groups
    ]


def joined(first, second):
    block = first.shape[0]
    none = jnp.zeros((block, block), F32)
    return jnp.concatenate(
        [jnp.concatenate([none, second], 1), jnp.concatenate([first, none], 1)], 0
    )


def pair_operators(refl_ref, keep, out_ref):
    block = refl_ref.shape[2]
    for g, (first, second, sfirst, ssecond, cross, q, p) in enumerate(pair_inverses(refl_ref, keep)):
        link = mm(mm(q, cross), p)
        solved_p = mm(p, sfirst)
        solved_q = mm(q, ssecond)
        reach = mm(link, sfirst)
        none = jnp.zeros((block, block), F32)
        solved = jnp.concatenate(
            [
                jnp.concatenate(
                    [-reach[:, :block], solved_q[:, :block] - reach[:, block:], solved_q[:, block:]], 1
                ),
                jnp.concatenate([solved_p, none], 1),
            ],
            0,
        )
        moved = mm(joined(first, second), solved, TN)
        row = lax.broadcasted_iota(jnp.int32, moved.shape, 0)
        col = lax.broadcasted_iota(jnp.int32, moved.shape, 1)
        out_ref[g] = jnp.where(row == col, 1.0, 0.0) - moved


def pair_action(refl_ref, keep, window):
    block = refl_ref.shape[2]
    cols = window.shape[1]
    ((first, second, sfirst, ssecond, cross, q, p),) = pair_inverses(refl_ref, keep)
    weights_p = jnp.concatenate([mm(sfirst, window[: 2 * block]), sfirst[:, :block]], 1)
    weights_q = mm(ssecond, window[block:])
    weights_q = jnp.concatenate([weights_q, jnp.zeros((block, block), F32)], 1)
    solved_p = mm(p, weights_p)
    solved_q = mm(q, weights_q - mm(cross, solved_p))
    moved = mm(joined(first, second), jnp.concatenate([solved_q, solved_p], 0), TN)
    row = lax.broadcasted_iota(jnp.int32, (3 * block, block), 0)
    col = lax.broadcasted_iota(jnp.int32, (3 * block, block), 1)
    return window - moved[:, :cols], jnp.where(row == col, 1.0, 0.0) - moved[:, cols:]


def pick_near(node, core, value):
    block = value.shape[0] // 3
    send_up = (core == 0) & ((node & 1) == 1)
    return jnp.where(send_up, value[:block], value[2 * block :])


def pick_far(node, value):
    block = value.shape[0] // 3
    return jnp.where((node & 2) == 0, value[2 * block :], value[:block])


def half_of(core, ref):
    rows = ref.shape[0] // PAIR
    return ref[pl.ds(pl.multiple_of(core * rows, rows), rows), :]


def assemble(place_ref, mine, theirs, groups, refl_ref):
    core, vec = place_ref[1], place_ref[2]
    rows = mine[0].shape[1]
    for step, (own, other) in enumerate(zip(mine, theirs)):
        at = pl.ds(pl.multiple_of((step ^ vec) * rows, rows), rows)
        for slot, group in enumerate(groups):
            refl_ref[core, slot, at, :] = own[group]
            refl_ref[1 - core, slot, at, :] = other[group]


def first_kernel(count, nodes, place_ref, *refs):
    mine, theirs = refs[:count], refs[count : 2 * count]
    top_ref, low_ref, near_ref, far_ref = refs[2 * count : 2 * count + 4]
    fixed_ref, lead_ref, out_near, out_far, refl_ref = refs[2 * count + 4 :]
    block = top_ref.shape[0]
    node, core = place_ref[0], place_ref[1]
    assemble(place_ref, mine, theirs, [0], refl_ref)
    below = jnp.where((node & 1) == 0, near_ref[...], far_ref[...])
    window = jnp.concatenate(
        [
            jnp.where(node == 0, top_ref[...], 0.0),
            low_ref[...],
            jnp.where(node == nodes - 1, 0.0, below),
        ],
        0,
    )
    fixed, lead = pair_action(refl_ref, node != nodes - 1, window)
    fixed_ref[...] = fixed
    lead_ref[...] = lead
    out_near[:block] = pick_near(node, core, fixed)
    out_near[block:] = pick_near(node, core, lead)
    out_far[...] = jnp.where(core == 0, pick_far(node, fixed), pick_far(node, lead))


def later_kernel(count, nodes, place_ref, *refs):
    mine, theirs = refs[:count], refs[count : 2 * count]
    oper_ref, map_ref, map_half, refl_ref = refs[2 * count :]
    node, core = place_ref[0], place_ref[1]
    later, size, _ = oper_ref.shape
    block = size // 3
    assemble(place_ref, mine, theirs, range(1, 1 + later), refl_ref)
    pair_operators(refl_ref, node != nodes - 1, oper_ref)
    if later != 2:
        return
    up, own, out = (slice(part * block, (part + 1) * block) for part in range(3))
    map_ref[:block] = oper_ref[0, out, :block]
    map_ref[block : 2 * block] = oper_ref[0, up, :block]
    map_ref[2 * block : 3 * block] = mm(oper_ref[1, out, own], oper_ref[0, own, :block])
    map_ref[3 * block : 4 * block] = oper_ref[1, out, out]
    map_ref[4 * block :] = oper_ref[1, out, :block]
    map_half[...] = half_of(core, map_ref)


def next_kernel(place_ref, near_ref, far_ref, near2_ref, far2_ref, fixed_ref, lead_ref, oper_ref, *outs):
    out_fixed, out_vec, out_half = outs
    block = far_ref.shape[0]
    node, core = place_ref[0], place_ref[1]
    here = core == 0
    odd, high = (node & 1) == 1, (node & 2) == 2
    near, near2, far, far2 = near_ref[...], near2_ref[...], far_ref[...], far2_ref[...]
    came1, map1 = (jnp.where(here, near[at], near2[at]) for at in (slice(0, block), slice(block, None)))
    came2, map2 = (jnp.where(here, near2[at], near[at]) for at in (slice(0, block), slice(block, None)))
    came3, map3 = jnp.where(here, far, far2), jnp.where(here, far2, far)
    carry = jnp.where(high, jnp.where(odd, came3, came2), came1)
    carry = jnp.where(node == 0, 0.0, carry)
    step = jnp.where(odd, came2, came3) + mm(jnp.where(odd, map2, map3), carry)
    carry = jnp.where(high, step, carry)
    step = came1 + mm(map1, carry)
    carry = jnp.where(node == 3, step, carry)
    up, own, out = (slice(part * block, (part + 1) * block) for part in range(3))
    fixed, lead = fixed_ref[...], lead_ref[...]
    cols = fixed.shape[1]
    none = jnp.zeros((block, block), F32)
    below = mm(jnp.where(odd, map3, map1), jnp.concatenate([fixed[out], lead[out]], 1))
    below += jnp.concatenate([jnp.where(odd, came3, came1), none], 1)
    window = jnp.concatenate(
        [
            jnp.concatenate([jnp.where(node == 0, fixed[up], 0.0), none], 1),
            jnp.concatenate([fixed[own], lead[own]], 1),
            jnp.where(node == 3, 0.0, below),
        ],
        0,
    )
    moved = mm(oper_ref[0], window)
    fixed = moved[:, :cols] + mm(moved[:, cols:], carry)
    out_fixed[...] = fixed
    out_vec[:block] = fixed[out]
    out_vec[block : 2 * block] = fixed[up]
    part = mm(oper_ref[1, out, own], fixed[own])
    first = mm(oper_ref[1, out, up], fixed[up])
    out_vec[2 * block :] = part + jnp.where(node == 0, first, 0.0)
    out_half[...] = half_of(core, out_vec)


def last_kernel(place_ref, *refs):
    vecs, maps, (fixed_ref, oper_ref, out_ref) = refs[:5], refs[5:10], refs[10:]
    block = out_ref.shape[0]
    own, out = slice(block, 2 * block), slice(2 * block, 3 * block)
    here = place_ref[1] == 0

    def either(one_ref, two_ref, first, last):
        return jnp.where(here, one_ref[first:last], two_ref[first:last])

    def fetch(arrays, mask, part):
        near_ref, far_ref, near2_ref, far2_ref, own_ref = arrays
        first, last = part * block, (part + 1) * block
        if mask == 0:
            return own_ref[first:last]
        if mask == 1:
            return either(near_ref, near2_ref, first, last)
        if mask == 2:
            return either(near2_ref, near_ref, first, last)
        half = far_ref.shape[0]
        pieces = []
        if first < half:
            pieces.append(either(far_ref, far2_ref, first, min(last, half)))
        if last > half:
            pieces.append(either(far2_ref, far_ref, max(first, half) - half, last - half))
        return jnp.concatenate(pieces, 0)

    def finish(node):
        offset = lambda pair, part: fetch(vecs, node ^ pair, part)
        matrix = lambda pair, part: fetch(maps, node ^ pair, part)
        at = pl.ds(pl.multiple_of(place_ref[1] * block, block), block)
        reach = min(node + 1, 3)
        carries = [None]
        for pair in range(reach):
            carry = offset(pair, 0)
            if pair:
                carry = carry + mm(matrix(pair, 0), carries[pair])
            carries.append(carry)
        belows = [
            offset(pair + 1, 1) + mm(matrix(pair + 1, 1), carries[pair + 1])
            for pair in range(reach)
        ]
        final = None
        for pair in range(node):
            end = mm(matrix(pair, 3), belows[pair])
            if pair:
                end = end + mm(matrix(pair, 2), carries[pair]) + mm(matrix(pair, 4), final)
            final = offset(pair, 2) + end
        reached = fixed_ref[: 2 * block]
        if node:
            reached = reached + mm(oper_ref[0, : 2 * block, :block], carries[node])
        else:
            final = reached[:block]
        total = mm(oper_ref[1, at, own], reached[own])
        if node < 3:
            total = total + mm(oper_ref[1, at, out], belows[node])
        out_ref[...] = total + mm(oper_ref[1, at, :block], final)

    for node in range(4):
        pl.when(place_ref[0] == node)(functools.partial(finish, node))


def call(kernel, outs, operands, scratch=(), work=0):
    vmem = pl.BlockSpec(memory_space=pltpu.VMEM)
    return pl.pallas_call(
        kernel,
        out_shape=[jax.ShapeDtypeStruct(shape, F32) for shape in outs],
        in_specs=[pl.BlockSpec(memory_space=pltpu.SMEM)] + [vmem] * (len(operands) - 1),
        out_specs=[vmem] * len(outs),
        scratch_shapes=list(scratch),
        cost_estimate=pl.CostEstimate(flops=work, bytes_accessed=0, transcendentals=0),
        compiler_params=pltpu.CompilerParams(vmem_limit_bytes=16 << 20),
    )(*operands)


def dot(left, right):
    return jnp.matmul(left, right, precision=lax.Precision.HIGHEST)


def spread(value, axis, size):
    if size & (size - 1) or size > 8:
        gathered = lax.all_gather(value, axis)
        return [gathered[place] for place in range(size)], False
    return [value] + [
        lax.ppermute(value, axis, [(place, place ^ mask) for place in range(size)])
        for mask in range(1, size)
    ], True


def many_pairs(fixed, lead, operators, node, nodes, row_count):
    groups, block = 1 + operators.shape[0], fixed.shape[0] // 3
    members = [[place * PAIR + core for place in range(nodes)] for core in range(PAIR)]
    for group in range(groups):
        down = jnp.concatenate([fixed[2 * block :], lead[2 * block :]], 0)
        up = jnp.concatenate([fixed[:block], lead[:block]], 0)
        earlier = lax.all_gather(down, "rows", axis_index_groups=members)
        later = lax.ppermute(
            up, "rows", [(place, place - PAIR) for place in range(PAIR, row_count)]
        )
        carry = jnp.zeros((block, fixed.shape[1]), F32)
        for place in range(nodes - 1):
            step = earlier[place, :block] + dot(earlier[place, block:], carry)
            carry = jnp.where(node > place, step, carry)
        result = fixed + dot(lead, carry)
        if group < groups - 1:
            below = later[:block] + dot(later[block:], result[2 * block :])
            window = jnp.concatenate(
                [
                    jnp.where(node == 0, result[:block], 0.0),
                    result[block : 2 * block],
                    jnp.where(node == nodes - 1, 0.0, below),
                ],
                0,
            )
            lead = operators[group][:, :block]
            fixed = dot(operators[group], window)
    return result


def local(vectors, reflectors):
    groups, _, _, window = reflectors.shape
    block = window // 2
    cols = vectors.shape[1]
    row_index = lax.axis_index("rows")
    row_count = lax.axis_size("rows")
    vec_index = lax.axis_index("vecs")
    vec_count = lax.axis_size("vecs")
    nodes = row_count // PAIR
    node = row_index // PAIR
    core = row_index % PAIR

    def swap(value, masks):
        moves = [
            (place, ((place // PAIR) ^ masks[place % PAIR]) * PAIR + place % PAIR)
            for place in range(row_count)
        ]
        return lax.ppermute(value, "rows", moves)

    def across(value):
        return lax.ppermute(value, "rows", [(place, place ^ 1) for place in range(row_count)])

    mine, mixed = spread(reflectors[:, 0], "vecs", vec_count)
    other = across(vectors)
    top = jnp.where(core == 0, vectors, other)
    low = jnp.where(core == 0, other, vectors)
    if nodes == 4:
        below = [swap(top, (1, 1)), swap(top, (3, 3))]
    else:
        below = [
            lax.ppermute(
                top, "rows", [(place, place - PAIR) for place in range(PAIR, row_count)]
            )
        ] * 2
    theirs = [across(piece) for piece in mine]
    mine[0] = jnp.where(vec_index < 0, 0.0, mine[0])
    place = jnp.stack([node, core, vec_index if mixed else 0]).astype(jnp.int32)
    hold = lax.optimization_barrier
    later = groups - 1
    size = 3 * block
    maps = 5 * block
    work = 16 * size**3
    pieces = [place, *mine, *theirs]
    fixed, lead, near, far = call(
        functools.partial(first_kernel, len(mine), nodes),
        [(size, cols), (size, block), (2 * block, cols), (block, cols)],
        [*pieces, top, low, *below],
        [pltpu.VMEM((PAIR, 1, block, window), F32)],
        work,
    )
    operators, sent, sent_half = call(
        functools.partial(later_kernel, len(mine), nodes),
        [(later, size, size), (maps, block), (maps // PAIR, block)],
        pieces,
        [pltpu.VMEM((PAIR, later, block, window), F32)],
        work * later,
    )
    if nodes != 4 or groups != 3:
        result = many_pairs(fixed, lead, operators, node, nodes, row_count)
        return jnp.where(core == 0, result[:block], result[block : 2 * block])

    def shared(near, far):
        return [place, near, far, across(near), across(far)]

    near, far = swap(near, (1, 2)), swap(far, (3, 3))
    near, far, sent, sent_half = hold((near, far, sent, sent_half))
    known = [swap(sent, (1, 2)), swap(sent_half, (3, 3))]
    fixed, vec, vec_half = call(
        next_kernel,
        [(size, cols), (size, cols), (size // PAIR, cols)],
        [*shared(near, far), fixed, lead, operators],
    )
    near, far = swap(vec, (1, 2)), swap(vec_half, (3, 3))
    far, *known = hold((far, *known))
    (result,) = call(
        last_kernel,
        [(block, cols)],
        [*shared(near, far), vec, *shared(*known)[1:], sent, fixed, operators],
    )
    return result


def solution(mesh):
    placed = (P("rows", "vecs"), P(None, "rows", "vecs", None))
    return jax.shard_map(
        local, mesh=mesh, in_specs=placed, out_specs=P("rows", "vecs"), check_vma=False
    )
```

```python
import functools
import jax
import jax.numpy as jnp
from jax import lax
from jax.experimental import pallas as pl
from jax.experimental.pallas import tpu as pltpu
from jax.sharding import PartitionSpec as P

PAIR = 2
F32, BF16 = jnp.float32, jnp.bfloat16
NN = ((1,), (0,))
NT = ((1,), (1,))
TN = ((0,), (0,))


def halves(value):
    high = value.astype(BF16)
    return high, (value - high.astype(F32)).astype(BF16)


def mm(left, right, dims=NN):
    left = left if isinstance(left, tuple) else halves(left)
    right = right if isinstance(right, tuple) else halves(right)

    (lc,), (rc,) = dims
    return lax.dot_general(
        jnp.concatenate([left[0], left[0], left[1]], lc),
        jnp.concatenate([right[0], right[1], right[0]], rc),
        (dims, ((), ())),
        preferred_element_type=F32,
    )


def same_block(shape, rows_block, cols_block, wrap):
    row = lax.broadcasted_iota(jnp.int32, shape, 0)
    col = lax.broadcasted_iota(jnp.int32, shape, 1)
    return (row // rows_block) == ((col % wrap) // cols_block)


def pair_inverses(refl_ref, keep):
    _, groups, block, window = refl_ref.shape
    wide = 2 * block
    groups = range(groups)
    firsts, seconds, sfirst, ssecond = [], [], [], []
    col = lax.broadcasted_iota(jnp.int32, (block, window), 1)
    for g in groups:
        a = refl_ref[0, g]
        b = jnp.where(keep | (col < block), refl_ref[1, g], 0.0)
        firsts.append(a)
        seconds.append(b)
        sfirst.append(a * (2.0 / jnp.sum(a * a, 1, keepdims=True)))
        ssecond.append(b * (2.0 / jnp.sum(b * b, 1, keepdims=True)))
    above = lax.broadcasted_iota(jnp.int32, (block, wide), 0) < (
        lax.broadcasted_iota(jnp.int32, (block, wide), 1) % block
    )
    near, cross = [], []
    for g in groups:
        ha = halves(firsts[g])
        gq = mm(ssecond[g], halves(seconds[g]), NT)
        gp = mm(sfirst[g], ha, NT)
        near.append(jnp.where(above, jnp.concatenate([gq, gp], 1), 0.0))
        cross.append(
            mm(ssecond[g][:, :block], (ha[0][:, block:], ha[1][:, block:]), NT)
        )

    def diagonal(value, size):
        mask = same_block((wide, wide), size, size, wide)
        return tuple(
            jnp.where(mask, jnp.concatenate([part] * (wide // size), 0), jnp.zeros((), BF16))
            for part in halves(value)
        )

    def gather_blocks(value, size):
        total = None
        for place in range(block // size):
            part = value[place * size : (place + 1) * size]
            pcol = lax.broadcasted_iota(jnp.int32, part.shape, 1)
            part = jnp.where((pcol % block) // size == place, part, 0.0)
            total = part if total is None else total + part
        return total

    def widen(value, size):
        old = value.shape[0]
        tall = jnp.concatenate([value] * (size // old), 0)
        return jnp.where(same_block(tall.shape, old, old, size), tall, 0.0)

    def quad(result, ring, size):
        across = [mm(r, diagonal(b, size)) for r, b in zip(result, ring)]
        halved = [halves(x) for x in across]
        once = [r - mm(x, diagonal(r, size)) for r, x in zip(result, halved)]
        square = [mm(h, diagonal(x, size)) for h, x in zip(halved, across)]
        return [o + mm(s, diagonal(o, size)) for o, s in zip(once, square)]

    small = [gather_blocks(n, 16) for n in near]
    shape = small[0].shape
    row = lax.broadcasted_iota(jnp.int32, shape, 0)
    scol = lax.broadcasted_iota(jnp.int32, shape, 1)
    eye = jnp.where(row == scol % 16, 1.0, 0.0)
    inner = (row // 4) == (scol % 16) // 4
    tiny = [jnp.where(inner, n, 0.0) for n in small]
    square = [mm(n, diagonal(n, 16)) for n in tiny]
    result = [eye - n for n in tiny]
    result = [r + mm(r, diagonal(s, 16)) for r, s in zip(result, square)]
    result = quad(result, [jnp.where(inner, 0.0, n) for n in small], 16)
    middle = [gather_blocks(n, 64) for n in near]
    mmask = same_block(middle[0].shape, 16, 16, 64)
    result = [widen(r, 64) for r in result]
    result = quad(result, [jnp.where(mmask, 0.0, n) for n in middle], 64)
    result = [widen(r, block) for r in result]
    bmask = same_block((block, wide), 64, 64, block)
    across = [mm(r, diagonal(jnp.where(bmask, 0.0, n), block)) for r, n in zip(result, near)]
    result = [r - mm(x, diagonal(r, block)) for r, x in zip(result, across)]
    return [
        (
            firsts[g],
            seconds[g],
            sfirst[g],
            ssecond[g],
            cross[g],
            halves(result[g][:, :block]),
            halves(result[g][:, block:]),
        )
        for g in groups
    ]


def joined(first, second):
    block = first.shape[0]
    none = jnp.zeros((block, block), F32)
    return jnp.concatenate(
        [jnp.concatenate([none, second], 1), jnp.concatenate([first, none], 1)], 0
    )


def whole_operator(parts, out_ref):
    first, second, sfirst, ssecond, cross, q, p = parts
    block = first.shape[0]
    link = mm(mm(q, cross), p)
    solved_p = mm(p, sfirst)
    solved_q = mm(q, ssecond)
    reach = mm(link, sfirst)
    none = jnp.zeros((block, block), F32)
    solved = jnp.concatenate(
        [
            jnp.concatenate(
                [-reach[:, :block], solved_q[:, :block] - reach[:, block:], solved_q[:, block:]], 1
            ),
            jnp.concatenate([solved_p, none], 1),
        ],
        0,
    )
    moved = mm(joined(first, second), solved, TN)
    row = lax.broadcasted_iota(jnp.int32, moved.shape, 0)
    col = lax.broadcasted_iota(jnp.int32, moved.shape, 1)
    out_ref[...] = jnp.where(row == col, 1.0, 0.0) - moved


def pair_action(parts, window):
    first, second, sfirst, ssecond, cross, q, p = parts
    block = first.shape[0]
    cols = window.shape[1]
    weights_p = jnp.concatenate([mm(sfirst, window[: 2 * block]), sfirst[:, :block]], 1)
    weights_q = mm(ssecond, window[block:])
    weights_q = jnp.concatenate([weights_q, jnp.zeros((block, block), F32)], 1)
    solved_p = mm(p, weights_p)
    solved_q = mm(q, weights_q - mm(cross, solved_p))
    moved = mm(joined(first, second), jnp.concatenate([solved_q, solved_p], 0), TN)
    row = lax.broadcasted_iota(jnp.int32, (3 * block, block), 0)
    col = lax.broadcasted_iota(jnp.int32, (3 * block, block), 1)
    return window - moved[:, :cols], jnp.where(row == col, 1.0, 0.0) - moved[:, cols:]


def pick_near(node, core, value):
    block = value.shape[0] // 3
    send_up = (core == 0) & ((node & 1) == 1)
    return jnp.where(send_up, value[:block], value[2 * block :])


def pick_far(node, value):
    block = value.shape[0] // 3
    return jnp.where((node & 2) == 0, value[2 * block :], value[:block])


def half_of(core, ref):
    rows = ref.shape[0] // PAIR
    return ref[pl.ds(pl.multiple_of(core * rows, rows), rows), :]


def first_kernel(count, nodes, place_ref, *refs):
    mine, theirs = refs[:count], refs[count : 2 * count]
    top_ref, low_ref, near_ref, far_ref = refs[2 * count : 2 * count + 4]
    fixed_ref, lead_ref, out_near, out_far, oper_ref, map_ref, map_half, refl_ref = refs[2 * count + 4 :]
    block = top_ref.shape[0]
    node, core, vec = place_ref[0], place_ref[1], place_ref[2]
    groups, rows, _ = mine[0].shape
    for step in range(count):
        at = pl.ds(pl.multiple_of((step ^ vec) * rows, rows), rows)
        for group in range(groups):
            refl_ref[core, group, at, :] = mine[step][group]
            refl_ref[1 - core, group, at, :] = theirs[step][group]
    parts = pair_inverses(refl_ref, node != nodes - 1)
    below = jnp.where((node & 1) == 0, near_ref[...], far_ref[...])
    window = jnp.concatenate(
        [
            jnp.where(node == 0, top_ref[...], 0.0),
            low_ref[...],
            jnp.where(node == nodes - 1, 0.0, below),
        ],
        0,
    )
    fixed, lead = pair_action(parts[0], window)
    fixed_ref[...] = fixed
    lead_ref[...] = lead
    out_near[:block] = pick_near(node, core, fixed)
    out_near[block:] = pick_near(node, core, lead)
    out_far[...] = jnp.where(core == 0, pick_far(node, fixed), pick_far(node, lead))
    for group in range(1, groups):
        whole_operator(parts[group], oper_ref.at[group - 1])
    if groups != 3:
        return
    up, own, out = (slice(part * block, (part + 1) * block) for part in range(3))
    map_ref[:block] = oper_ref[0, out, :block]
    map_ref[block : 2 * block] = oper_ref[0, up, :block]
    map_ref[2 * block : 3 * block] = mm(oper_ref[1, out, own], oper_ref[0, own, :block])
    map_ref[3 * block : 4 * block] = oper_ref[1, out, out]
    map_ref[4 * block :] = oper_ref[1, out, :block]
    map_half[...] = half_of(core, map_ref)


def between_kernel(place_ref, fixed_ref, lead_ref, oper_ref, base_ref, onto_ref):
    block = fixed_ref.shape[0] // 3
    own = slice(block, 2 * block)
    first = jnp.where(place_ref[0] == 0, fixed_ref[:block], 0.0)
    operator = oper_ref.at[0]
    base_ref[...] = mm(
        operator[:, : 2 * block], jnp.concatenate([first, fixed_ref[own]], 0)
    )
    onto_ref[...] = mm(operator[:, own], lead_ref[own])


def next_kernel(place_ref, near_ref, far_ref, near2_ref, far2_ref, fixed_ref, lead_ref, oper_ref, base_ref, onto_ref, *outs):
    out_fixed, out_vec, out_half = outs
    block = far_ref.shape[0]
    node, core = place_ref[0], place_ref[1]
    here = core == 0
    odd, high = (node & 1) == 1, (node & 2) == 2
    near, near2, far, far2 = near_ref[...], near2_ref[...], far_ref[...], far2_ref[...]
    came1, map1 = (jnp.where(here, near[at], near2[at]) for at in (slice(0, block), slice(block, None)))
    came2, map2 = (jnp.where(here, near2[at], near[at]) for at in (slice(0, block), slice(block, None)))
    came3, map3 = jnp.where(here, far, far2), jnp.where(here, far2, far)
    carry = jnp.where(high, jnp.where(odd, came3, came2), came1)
    carry = jnp.where(node == 0, 0.0, carry)
    step = jnp.where(odd, came2, came3) + mm(jnp.where(odd, map2, map3), carry)
    carry = jnp.where(high, step, carry)
    step = came1 + mm(map1, carry)
    carry = jnp.where(node == 3, step, carry)
    up, own, out = (slice(part * block, (part + 1) * block) for part in range(3))
    cols = carry.shape[1]
    reach = mm(
        jnp.where(odd, map3, map1), jnp.concatenate([fixed_ref[out], lead_ref[out]], 1)
    )
    below = jnp.where(odd, came3, came1) + reach[:, :cols] + mm(reach[:, cols:], carry)
    below = jnp.where(node == 3, 0.0, below)
    fixed = base_ref[...] + mm(
        jnp.concatenate([oper_ref[0, :, out], onto_ref[...]], 1),
        jnp.concatenate([below, carry], 0),
    )
    out_fixed[...] = fixed
    out_vec[:block] = fixed[out]
    out_vec[block : 2 * block] = fixed[up]
    first = jnp.where(node == 0, fixed[up], 0.0)
    out_vec[2 * block :] = mm(
        oper_ref[1, out, : 2 * block], jnp.concatenate([first, fixed[own]], 0)
    )
    out_half[...] = half_of(core, out_vec)


def last_kernel(place_ref, *refs):
    vecs, maps, (fixed_ref, oper_ref, out_ref) = refs[:5], refs[5:10], refs[10:]
    block = out_ref.shape[0]
    own, out = slice(block, 2 * block), slice(2 * block, 3 * block)
    here = place_ref[1] == 0

    def either(one_ref, two_ref, first, last):
        return jnp.where(here, one_ref[first:last], two_ref[first:last])

    def fetch(arrays, mask, part):
        near_ref, far_ref, near2_ref, far2_ref, own_ref = arrays
        first, last = part * block, (part + 1) * block
        if mask == 0:
            return own_ref[first:last]
        if mask == 1:
            return either(near_ref, near2_ref, first, last)
        if mask == 2:
            return either(near2_ref, near_ref, first, last)
        half = far_ref.shape[0]
        pieces = []
        if first < half:
            pieces.append(either(far_ref, far2_ref, first, min(last, half)))
        if last > half:
            pieces.append(either(far2_ref, far_ref, max(first, half) - half, last - half))
        return jnp.concatenate(pieces, 0)

    def finish(node):
        offset = lambda pair, part: fetch(vecs, node ^ pair, part)
        matrix = lambda pair, part: fetch(maps, node ^ pair, part)
        at = pl.ds(pl.multiple_of(place_ref[1] * block, block), block)
        reach = min(node + 1, 3)
        carries = [None]
        for pair in range(reach):
            carry = offset(pair, 0)
            if pair:
                carry = carry + mm(matrix(pair, 0), carries[pair])
            carries.append(carry)
        belows = [
            offset(pair + 1, 1) + mm(matrix(pair + 1, 1), carries[pair + 1])
            for pair in range(reach)
        ]
        final = None
        for pair in range(node):
            end = mm(matrix(pair, 3), belows[pair])
            if pair:
                end = end + mm(matrix(pair, 2), carries[pair]) + mm(matrix(pair, 4), final)
            final = offset(pair, 2) + end
        reached = fixed_ref[: 2 * block]
        if node:
            reached = reached + mm(oper_ref[0, : 2 * block, :block], carries[node])
        else:
            final = reached[:block]
        total = mm(oper_ref[1, at, own], reached[own])
        if node < 3:
            total = total + mm(oper_ref[1, at, out], belows[node])
        out_ref[...] = total + mm(oper_ref[1, at, :block], final)

    for node in range(4):
        pl.when(place_ref[0] == node)(functools.partial(finish, node))


def call(kernel, outs, operands, scratch=(), work=0):
    vmem = pl.BlockSpec(memory_space=pltpu.VMEM)
    return pl.pallas_call(
        kernel,
        out_shape=[jax.ShapeDtypeStruct(shape, F32) for shape in outs],
        in_specs=[pl.BlockSpec(memory_space=pltpu.SMEM)] + [vmem] * (len(operands) - 1),
        out_specs=[vmem] * len(outs),
        scratch_shapes=list(scratch),
        cost_estimate=pl.CostEstimate(flops=work, bytes_accessed=0, transcendentals=0),
        compiler_params=pltpu.CompilerParams(vmem_limit_bytes=16 << 20),
    )(*operands)


def dot(left, right):
    return jnp.matmul(left, right, precision=lax.Precision.HIGHEST)


def spread(value, axis, size):
    if size & (size - 1) or size > 8:
        gathered = lax.all_gather(value, axis)
        return [gathered[place] for place in range(size)], False
    return [value] + [
        lax.ppermute(value, axis, [(place, place ^ mask) for place in range(size)])
        for mask in range(1, size)
    ], True


def many_pairs(fixed, lead, operators, node, nodes, row_count):
    groups, block = 1 + operators.shape[0], fixed.shape[0] // 3
    members = [[place * PAIR + core for place in range(nodes)] for core in range(PAIR)]
    for group in range(groups):
        down = jnp.concatenate([fixed[2 * block :], lead[2 * block :]], 0)
        up = jnp.concatenate([fixed[:block], lead[:block]], 0)
        earlier = lax.all_gather(down, "rows", axis_index_groups=members)
        later = lax.ppermute(
            up, "rows", [(place, place - PAIR) for place in range(PAIR, row_count)]
        )
        carry = jnp.zeros((block, fixed.shape[1]), F32)
        for place in range(nodes - 1):
            step = earlier[place, :block] + dot(earlier[place, block:], carry)
            carry = jnp.where(node > place, step, carry)
        result = fixed + dot(lead, carry)
        if group < groups - 1:
            below = later[:block] + dot(later[block:], result[2 * block :])
            window = jnp.concatenate(
                [
                    jnp.where(node == 0, result[:block], 0.0),
                    result[block : 2 * block],
                    jnp.where(node == nodes - 1, 0.0, below),
                ],
                0,
            )
            lead = operators[group][:, :block]
            fixed = dot(operators[group], window)
    return result


def local(vectors, reflectors):
    groups, _, _, window = reflectors.shape
    block = window // 2
    cols = vectors.shape[1]
    row_index = lax.axis_index("rows")
    row_count = lax.axis_size("rows")
    vec_index = lax.axis_index("vecs")
    vec_count = lax.axis_size("vecs")
    nodes = row_count // PAIR
    node = row_index // PAIR
    core = row_index % PAIR

    def swap(value, masks):
        moves = [
            (place, ((place // PAIR) ^ masks[place % PAIR]) * PAIR + place % PAIR)
            for place in range(row_count)
        ]
        return lax.ppermute(value, "rows", moves)

    def across(value):
        return lax.ppermute(value, "rows", [(place, place ^ 1) for place in range(row_count)])

    mine, mixed = spread(reflectors[:, 0], "vecs", vec_count)
    other = across(vectors)
    top = jnp.where(core == 0, vectors, other)
    low = jnp.where(core == 0, other, vectors)
    if nodes == 4:
        below = [swap(top, (1, 1)), swap(top, (3, 3))]
    else:
        below = [
            lax.ppermute(
                top, "rows", [(place, place - PAIR) for place in range(PAIR, row_count)]
            )
        ] * 2
    theirs = [across(piece) for piece in mine]
    mine[0] = jnp.where(vec_index < 0, 0.0, mine[0])
    place = jnp.stack([node, core, vec_index if mixed else 0]).astype(jnp.int32)
    hold = lax.optimization_barrier
    later = groups - 1
    size = 3 * block
    maps = 5 * block
    fixed, lead, near, far, operators, sent, sent_half = call(
        functools.partial(first_kernel, len(mine), nodes),
        [
            (size, cols),
            (size, block),
            (2 * block, cols),
            (block, cols),
            (later, size, size),
            (maps, block),
            (maps // PAIR, block),
        ],
        [place, *mine, *theirs, top, low, *below],
        [pltpu.VMEM((PAIR, groups, block, window), F32)],
    )
    if nodes != 4 or groups != 3:
        result = many_pairs(fixed, lead, operators, node, nodes, row_count)
        return jnp.where(core == 0, result[:block], result[block : 2 * block])

    def shared(near, far):
        return [place, near, far, across(near), across(far)]

    base, onto = call(
        between_kernel,
        [(size, cols), (size, block)],
        [place, fixed, lead, operators],
        work=32 * size**3,
    )
    near, far = swap(near, (1, 2)), swap(far, (3, 3))
    near, far, base = hold((near, far, base))
    known = [swap(sent, (1, 2)), swap(sent_half, (3, 3))]
    fixed, vec, vec_half = call(
        next_kernel,
        [(size, cols), (size, cols), (size // PAIR, cols)],
        [*shared(near, far), fixed, lead, operators, base, onto],
    )
    near, far = swap(vec, (1, 2)), swap(vec_half, (3, 3))
    far, *known = hold((far, *known))
    (result,) = call(
        last_kernel,
        [(block, cols)],
        [*shared(near, far), vec, *shared(*known)[1:], sent, fixed, operators],
    )
    return result


def solution(mesh):
    placed = (P("rows", "vecs"), P(None, "rows", "vecs", None))
    return jax.shard_map(
        local, mesh=mesh, in_specs=placed, out_specs=P("rows", "vecs"), check_vma=False
    )
```

```python
import functools
import jax
import jax.numpy as jnp
from jax import lax
from jax.experimental import pallas as pl
from jax.experimental.pallas import tpu as pltpu
from jax.sharding import PartitionSpec as P

PAIR = 2
F32, BF16 = jnp.float32, jnp.bfloat16
NN = ((1,), (0,))
NT = ((1,), (1,))
TN = ((0,), (0,))


def halves(value):
    high = value.astype(BF16)
    return high, (value - high.astype(F32)).astype(BF16)


def mm(left, right, dims=NN):
    left = left if isinstance(left, tuple) else halves(left)
    right = right if isinstance(right, tuple) else halves(right)

    (lc,), (rc,) = dims
    return lax.dot_general(
        jnp.concatenate([left[0], left[0], left[1]], lc),
        jnp.concatenate([right[0], right[1], right[0]], rc),
        (dims, ((), ())),
        preferred_element_type=F32,
    )


def same_block(shape, rows_block, cols_block, wrap):
    row = lax.broadcasted_iota(jnp.int32, shape, 0)
    col = lax.broadcasted_iota(jnp.int32, shape, 1)
    return (row // rows_block) == ((col % wrap) // cols_block)


def pair_inverses(refl_ref, keep):
    _, groups, block, window = refl_ref.shape
    wide = 2 * block
    groups = range(groups)
    firsts, seconds, sfirst, ssecond = [], [], [], []
    col = lax.broadcasted_iota(jnp.int32, (block, window), 1)
    for g in groups:
        a = refl_ref[0, g]
        b = jnp.where(keep | (col < block), refl_ref[1, g], 0.0)
        firsts.append(a)
        seconds.append(b)
        sfirst.append(a * (2.0 / jnp.sum(a * a, 1, keepdims=True)))
        ssecond.append(b * (2.0 / jnp.sum(b * b, 1, keepdims=True)))
    above = lax.broadcasted_iota(jnp.int32, (block, wide), 0) < (
        lax.broadcasted_iota(jnp.int32, (block, wide), 1) % block
    )
    near, cross = [], []
    for g in groups:
        ha = halves(firsts[g])
        gq = mm(ssecond[g], halves(seconds[g]), NT)
        gp = mm(sfirst[g], ha, NT)
        near.append(jnp.where(above, jnp.concatenate([gq, gp], 1), 0.0))
        cross.append(
            mm(ssecond[g][:, :block], (ha[0][:, block:], ha[1][:, block:]), NT)
        )

    def diagonal(value, size):
        mask = same_block((wide, wide), size, size, wide)
        return tuple(
            jnp.where(mask, jnp.concatenate([part] * (wide // size), 0), jnp.zeros((), BF16))
            for part in halves(value)
        )

    def gather_blocks(value, size):
        total = None
        for place in range(block // size):
            part = value[place * size : (place + 1) * size]
            pcol = lax.broadcasted_iota(jnp.int32, part.shape, 1)
            part = jnp.where((pcol % block) // size == place, part, 0.0)
            total = part if total is None else total + part
        return total

    def widen(value, size):
        old = value.shape[0]
        tall = jnp.concatenate([value] * (size // old), 0)
        return jnp.where(same_block(tall.shape, old, old, size), tall, 0.0)

    def quad(result, ring, size):
        across = [mm(r, diagonal(b, size)) for r, b in zip(result, ring)]
        halved = [halves(x) for x in across]
        once = [r - mm(x, diagonal(r, size)) for r, x in zip(result, halved)]
        square = [mm(h, diagonal(x, size)) for h, x in zip(halved, across)]
        return [o + mm(s, diagonal(o, size)) for o, s in zip(once, square)]

    small = [gather_blocks(n, 16) for n in near]
    shape = small[0].shape
    row = lax.broadcasted_iota(jnp.int32, shape, 0)
    scol = lax.broadcasted_iota(jnp.int32, shape, 1)
    eye = jnp.where(row == scol % 16, 1.0, 0.0)
    inner = (row // 4) == (scol % 16) // 4
    tiny = [jnp.where(inner, n, 0.0) for n in small]
    square = [mm(n, diagonal(n, 16)) for n in tiny]
    result = [eye - n for n in tiny]
    result = [r + mm(r, diagonal(s, 16)) for r, s in zip(result, square)]
    result = quad(result, [jnp.where(inner, 0.0, n) for n in small], 16)
    middle = [gather_blocks(n, 64) for n in near]
    mmask = same_block(middle[0].shape, 16, 16, 64)
    result = [widen(r, 64) for r in result]
    result = quad(result, [jnp.where(mmask, 0.0, n) for n in middle], 64)
    result = [widen(r, block) for r in result]
    bmask = same_block((block, wide), 64, 64, block)
    across = [mm(r, diagonal(jnp.where(bmask, 0.0, n), block)) for r, n in zip(result, near)]
    result = [r - mm(x, diagonal(r, block)) for r, x in zip(result, across)]
    return [
        (
            firsts[g],
            seconds[g],
            sfirst[g],
            ssecond[g],
            cross[g],
            result[g][:, :block],
            result[g][:, block:],
        )
        for g in groups
    ]


def joined(first, second):
    block = first.shape[0]
    none = jnp.zeros((block, block), F32)
    return jnp.concatenate(
        [jnp.concatenate([none, second], 1), jnp.concatenate([first, none], 1)], 0
    )


def whole_operator(parts, out_ref):
    first, second, sfirst, ssecond, cross, q, p = parts
    q, p = halves(q), halves(p)
    block = first.shape[0]
    link = mm(mm(q, cross), p)
    solved_p = mm(p, sfirst)
    solved_q = mm(q, ssecond)
    reach = mm(link, sfirst)
    none = jnp.zeros((block, block), F32)
    solved = jnp.concatenate(
        [
            jnp.concatenate(
                [-reach[:, :block], solved_q[:, :block] - reach[:, block:], solved_q[:, block:]], 1
            ),
            jnp.concatenate([solved_p, none], 1),
        ],
        0,
    )
    top = mm(first[:, :block], solved[block:, : 2 * block], TN)
    both = jnp.concatenate([second[:, :block], first[:, block:]], 0)
    moved = jnp.concatenate(
        [
            jnp.concatenate([top, none], 1),
            mm(both, solved, TN),
            mm(second[:, block:], solved[:block], TN),
        ],
        0,
    )
    row = lax.broadcasted_iota(jnp.int32, moved.shape, 0)
    col = lax.broadcasted_iota(jnp.int32, moved.shape, 1)
    out_ref[...] = jnp.where(row == col, 1.0, 0.0) - moved


def pair_action(parts, window):
    first, second, sfirst, ssecond, cross, q, p = parts
    q, p = halves(q), halves(p)
    block = first.shape[0]
    cols = window.shape[1]
    weights_p = jnp.concatenate([mm(sfirst, window[: 2 * block]), sfirst[:, :block]], 1)
    weights_q = mm(ssecond, window[block:])
    weights_q = jnp.concatenate([weights_q, jnp.zeros((block, block), F32)], 1)
    solved_p = mm(p, weights_p)
    solved_q = mm(q, weights_q - mm(cross, solved_p))
    moved = mm(joined(first, second), jnp.concatenate([solved_q, solved_p], 0), TN)
    row = lax.broadcasted_iota(jnp.int32, (3 * block, block), 0)
    col = lax.broadcasted_iota(jnp.int32, (3 * block, block), 1)
    return window - moved[:, :cols], jnp.where(row == col, 1.0, 0.0) - moved[:, cols:]


def pick_near(node, core, value):
    block = value.shape[0] // 3
    send_up = (core == 0) & ((node & 1) == 1)
    return jnp.where(send_up, value[:block], value[2 * block :])


def pick_far(node, value):
    block = value.shape[0] // 3
    return jnp.where((node & 2) == 0, value[2 * block :], value[:block])


def half_of(core, ref):
    rows = ref.shape[0] // PAIR
    return ref[pl.ds(pl.multiple_of(core * rows, rows), rows), :]


def first_kernel(count, nodes, place_ref, *refs):
    mine, theirs = refs[:count], refs[count : 2 * count]
    top_ref, low_ref, near_ref, far_ref = refs[2 * count : 2 * count + 4]
    (fixed_ref, lead_ref, out_near, out_far), keep_refs = refs[2 * count + 4 : 2 * count + 8], refs[2 * count + 8 : -1]
    refl_ref = refs[-1]
    block = top_ref.shape[0]
    node, core, vec = place_ref[0], place_ref[1], place_ref[2]
    groups, rows, _ = mine[0].shape
    for step in range(count):
        at = pl.ds(pl.multiple_of((step ^ vec) * rows, rows), rows)
        for group in range(groups):
            refl_ref[core, group, at, :] = mine[step][group]
            refl_ref[1 - core, group, at, :] = theirs[step][group]
    parts = pair_inverses(refl_ref, node != nodes - 1)
    below = jnp.where((node & 1) == 0, near_ref[...], far_ref[...])
    window = jnp.concatenate(
        [
            jnp.where(node == 0, top_ref[...], 0.0),
            low_ref[...],
            jnp.where(node == nodes - 1, 0.0, below),
        ],
        0,
    )
    fixed, lead = pair_action(parts[0], window)
    fixed_ref[...] = fixed
    lead_ref[...] = lead
    out_near[:block] = pick_near(node, core, fixed)
    out_near[block:] = pick_near(node, core, lead)
    out_far[...] = jnp.where(core == 0, pick_far(node, fixed), pick_far(node, lead))
    for group in range(1, groups):
        for part, array in enumerate(parts[group]):
            keep_refs[part][group - 1] = array


def later_kernel(place_ref, *refs):
    parts, (oper_ref, map_ref, map_half) = refs[:7], refs[7:]
    core = place_ref[1]
    later, size, _ = oper_ref.shape
    block = size // 3
    for group in range(later):
        whole_operator([part[group] for part in parts], oper_ref.at[group])
    if later != 2:
        return
    up, own, out = (slice(part * block, (part + 1) * block) for part in range(3))
    map_ref[:block] = oper_ref[0, out, :block]
    map_ref[block : 2 * block] = oper_ref[0, up, :block]
    map_ref[2 * block : 3 * block] = mm(oper_ref[1, out, own], oper_ref[0, own, :block])
    map_ref[3 * block : 4 * block] = oper_ref[1, out, out]
    map_ref[4 * block :] = oper_ref[1, out, :block]
    map_half[...] = half_of(core, map_ref)


def between_kernel(place_ref, fixed_ref, lead_ref, oper_ref, base_ref, onto_ref):
    block = fixed_ref.shape[0] // 3
    own = slice(block, 2 * block)
    first = jnp.where(place_ref[0] == 0, fixed_ref[:block], 0.0)
    operator = oper_ref.at[0]
    base = mm(operator[:, : 2 * block], jnp.concatenate([first, fixed_ref[own]], 0))
    onto = jnp.concatenate([operator[:, 2 * block :], mm(operator[:, own], lead_ref[own])], 1)
    rows = oper_ref[1, 2 * block :, : 2 * block]
    cols = base.shape[1]
    both = jnp.concatenate([base[: 2 * block], onto[: 2 * block]], 1)
    both = jnp.concatenate([jnp.where(place_ref[0] == 0, both[:block], 0.0), both[block:]], 0)
    both = mm(rows, both)
    base_ref[: 3 * block] = base
    base_ref[3 * block :] = both[:, :cols]
    onto_ref[: 3 * block] = onto
    onto_ref[3 * block :] = both[:, cols:]


def next_kernel(place_ref, near_ref, far_ref, near2_ref, far2_ref, fixed_ref, lead_ref, base_ref, onto_ref, *outs):
    out_fixed, out_vec, out_half = outs
    block = far_ref.shape[0]
    node, core = place_ref[0], place_ref[1]
    here = core == 0
    odd, high = (node & 1) == 1, (node & 2) == 2
    near, near2, far, far2 = near_ref[...], near2_ref[...], far_ref[...], far2_ref[...]
    came1, map1 = (jnp.where(here, near[at], near2[at]) for at in (slice(0, block), slice(block, None)))
    came2, map2 = (jnp.where(here, near2[at], near[at]) for at in (slice(0, block), slice(block, None)))
    came3, map3 = jnp.where(here, far, far2), jnp.where(here, far2, far)
    carry = jnp.where(high, jnp.where(odd, came3, came2), came1)
    carry = jnp.where(node == 0, 0.0, carry)
    step = jnp.where(odd, came2, came3) + mm(jnp.where(odd, map2, map3), carry)
    carry = jnp.where(high, step, carry)
    step = came1 + mm(map1, carry)
    carry = jnp.where(node == 3, step, carry)
    up, own, out = (slice(part * block, (part + 1) * block) for part in range(3))
    cols = carry.shape[1]
    reach = mm(
        jnp.where(odd, map3, map1), jnp.concatenate([fixed_ref[out], lead_ref[out]], 1)
    )
    below = jnp.where(odd, came3, came1) + reach[:, :cols] + mm(reach[:, cols:], carry)
    below = jnp.where(node == 3, 0.0, below)
    fixed = base_ref[...] + mm(onto_ref[...], jnp.concatenate([below, carry], 0))
    out_fixed[...] = fixed[: 3 * block]
    out_vec[:block] = fixed[out]
    out_vec[block : 2 * block] = fixed[up]
    out_vec[2 * block :] = fixed[3 * block :]
    out_half[...] = half_of(core, out_vec)


def last_kernel(place_ref, *refs):
    vecs, maps, (fixed_ref, oper_ref, out_ref) = refs[:5], refs[5:10], refs[10:]
    block = out_ref.shape[0]
    own, out = slice(block, 2 * block), slice(2 * block, 3 * block)
    here = place_ref[1] == 0

    def either(one_ref, two_ref, first, last):
        return jnp.where(here, one_ref[first:last], two_ref[first:last])

    def fetch(arrays, mask, part):
        near_ref, far_ref, near2_ref, far2_ref, own_ref = arrays
        first, last = part * block, (part + 1) * block
        if mask == 0:
            return own_ref[first:last]
        if mask == 1:
            return either(near_ref, near2_ref, first, last)
        if mask == 2:
            return either(near2_ref, near_ref, first, last)
        half = far_ref.shape[0]
        pieces = []
        if first < half:
            pieces.append(either(far_ref, far2_ref, first, min(last, half)))
        if last > half:
            pieces.append(either(far2_ref, far_ref, max(first, half) - half, last - half))
        return jnp.concatenate(pieces, 0)

    def finish(node):
        offset = lambda pair, part: fetch(vecs, node ^ pair, part)
        matrix = lambda pair, part: fetch(maps, node ^ pair, part)
        at = pl.ds(pl.multiple_of(place_ref[1] * block, block), block)
        reach = min(node + 1, 3)
        carries = [None]
        for pair in range(reach):
            carry = offset(pair, 0)
            if pair:
                carry = carry + mm(matrix(pair, 0), carries[pair])
            carries.append(carry)
        belows = [
            offset(pair + 1, 1) + mm(matrix(pair + 1, 1), carries[pair + 1])
            for pair in range(reach)
        ]
        final = None
        for pair in range(node):
            end = mm(matrix(pair, 3), belows[pair])
            if pair:
                end = end + mm(matrix(pair, 2), carries[pair]) + mm(matrix(pair, 4), final)
            final = offset(pair, 2) + end
        reached = fixed_ref[: 2 * block]
        if node:
            reached = reached + mm(oper_ref[0, : 2 * block, :block], carries[node])
        else:
            final = reached[:block]
        total = mm(oper_ref[1, at, own], reached[own])
        if node < 3:
            total = total + mm(oper_ref[1, at, out], belows[node])
        out_ref[...] = total + mm(oper_ref[1, at, :block], final)

    for node in range(4):
        pl.when(place_ref[0] == node)(functools.partial(finish, node))


def call(kernel, outs, operands, scratch=(), work=0):
    vmem = pl.BlockSpec(memory_space=pltpu.VMEM)
    return pl.pallas_call(
        kernel,
        out_shape=[jax.ShapeDtypeStruct(shape, F32) for shape in outs],
        in_specs=[pl.BlockSpec(memory_space=pltpu.SMEM)] + [vmem] * (len(operands) - 1),
        out_specs=[vmem] * len(outs),
        scratch_shapes=list(scratch),
        cost_estimate=pl.CostEstimate(flops=work, bytes_accessed=0, transcendentals=0),
        compiler_params=pltpu.CompilerParams(vmem_limit_bytes=16 << 20),
    )(*operands)


def dot(left, right):
    return jnp.matmul(left, right, precision=lax.Precision.HIGHEST)


def spread(value, axis, size):
    if size & (size - 1) or size > 8:
        gathered = lax.all_gather(value, axis)
        return [gathered[place] for place in range(size)], False
    return [value] + [
        lax.ppermute(value, axis, [(place, place ^ mask) for place in range(size)])
        for mask in range(1, size)
    ], True


def many_pairs(fixed, lead, operators, node, nodes, row_count):
    groups, block = 1 + operators.shape[0], fixed.shape[0] // 3
    members = [[place * PAIR + core for place in range(nodes)] for core in range(PAIR)]
    for group in range(groups):
        down = jnp.concatenate([fixed[2 * block :], lead[2 * block :]], 0)
        up = jnp.concatenate([fixed[:block], lead[:block]], 0)
        earlier = lax.all_gather(down, "rows", axis_index_groups=members)
        later = lax.ppermute(
            up, "rows", [(place, place - PAIR) for place in range(PAIR, row_count)]
        )
        carry = jnp.zeros((block, fixed.shape[1]), F32)
        for place in range(nodes - 1):
            step = earlier[place, :block] + dot(earlier[place, block:], carry)
            carry = jnp.where(node > place, step, carry)
        result = fixed + dot(lead, carry)
        if group < groups - 1:
            below = later[:block] + dot(later[block:], result[2 * block :])
            window = jnp.concatenate(
                [
                    jnp.where(node == 0, result[:block], 0.0),
                    result[block : 2 * block],
                    jnp.where(node == nodes - 1, 0.0, below),
                ],
                0,
            )
            lead = operators[group][:, :block]
            fixed = dot(operators[group], window)
    return result


def local(vectors, reflectors):
    groups, _, _, window = reflectors.shape
    block = window // 2
    cols = vectors.shape[1]
    row_index = lax.axis_index("rows")
    row_count = lax.axis_size("rows")
    vec_index = lax.axis_index("vecs")
    vec_count = lax.axis_size("vecs")
    nodes = row_count // PAIR
    node = row_index // PAIR
    core = row_index % PAIR

    def swap(value, masks):
        moves = [
            (place, ((place // PAIR) ^ masks[place % PAIR]) * PAIR + place % PAIR)
            for place in range(row_count)
        ]
        return lax.ppermute(value, "rows", moves)

    def across(value):
        return lax.ppermute(value, "rows", [(place, place ^ 1) for place in range(row_count)])

    mine, mixed = spread(reflectors[:, 0], "vecs", vec_count)
    other = across(vectors)
    top = jnp.where(core == 0, vectors, other)
    low = jnp.where(core == 0, other, vectors)
    if nodes == 4:
        below = [swap(top, (1, 1)), swap(top, (3, 3))]
    else:
        below = [
            lax.ppermute(
                top, "rows", [(place, place - PAIR) for place in range(PAIR, row_count)]
            )
        ] * 2
    theirs = [across(piece) for piece in mine]
    mine[0] = jnp.where(vec_index < 0, 0.0, mine[0])
    place = jnp.stack([node, core, vec_index if mixed else 0]).astype(jnp.int32)
    hold = lax.optimization_barrier
    later = groups - 1
    size = 3 * block
    maps = 5 * block
    fixed, lead, near, far, *parts = call(
        functools.partial(first_kernel, len(mine), nodes),
        [
            (size, cols),
            (size, block),
            (2 * block, cols),
            (block, cols),
            *[(later, block, window)] * 4,
            *[(later, block, block)] * 3,
        ],
        [place, *mine, *theirs, top, low, *below],
        [pltpu.VMEM((PAIR, groups, block, window), F32)],
    )
    operators, sent, sent_half = call(
        later_kernel,
        [(later, size, size), (maps, block), (maps // PAIR, block)],
        [place, *parts],
        work=32 * size**3,
    )
    if nodes != 4 or groups != 3:
        result = many_pairs(fixed, lead, operators, node, nodes, row_count)
        return jnp.where(core == 0, result[:block], result[block : 2 * block])

    def shared(near, far):
        return [place, near, far, across(near), across(far)]

    base, onto = call(
        between_kernel,
        [(4 * block, cols), (4 * block, 2 * block)],
        [place, fixed, lead, operators],
        work=32 * size**3,
    )
    near, far = swap(near, (1, 2)), swap(far, (3, 3))
    near, far, base = hold((near, far, base))
    known = [swap(sent, (1, 2)), swap(sent_half, (3, 3))]
    fixed, vec, vec_half = call(
        next_kernel,
        [(size, cols), (size, cols), (size // PAIR, cols)],
        [*shared(near, far), fixed, lead, base, onto],
    )
    near, far = swap(vec, (1, 2)), swap(vec_half, (3, 3))
    far, *known = hold((far, *known))
    (result,) = call(
        last_kernel,
        [(block, cols)],
        [*shared(near, far), vec, *shared(*known)[1:], sent, fixed, operators],
    )
    return result


def solution(mesh):
    placed = (P("rows", "vecs"), P(None, "rows", "vecs", None))
    return jax.shard_map(
        local, mesh=mesh, in_specs=placed, out_specs=P("rows", "vecs"), check_vma=False
    )
```

```python
import functools
import jax
import jax.numpy as jnp
from jax import lax
from jax.experimental import pallas as pl
from jax.experimental.pallas import tpu as pltpu
from jax.sharding import PartitionSpec as P

PAIR = 2
F32, BF16 = jnp.float32, jnp.bfloat16
NN = ((1,), (0,))
NT = ((1,), (1,))
TN = ((0,), (0,))


def halves(value):
    high = value.astype(BF16)
    return high, (value - high.astype(F32)).astype(BF16)


def mm(left, right, dims=NN):
    left = left if isinstance(left, tuple) else halves(left)
    right = right if isinstance(right, tuple) else halves(right)

    (lc,), (rc,) = dims
    return lax.dot_general(
        jnp.concatenate([left[0], left[0], left[1]], lc),
        jnp.concatenate([right[0], right[1], right[0]], rc),
        (dims, ((), ())),
        preferred_element_type=F32,
    )


def same_block(shape, rows_block, cols_block, wrap):
    row = lax.broadcasted_iota(jnp.int32, shape, 0)
    col = lax.broadcasted_iota(jnp.int32, shape, 1)
    return (row // rows_block) == ((col % wrap) // cols_block)


def pair_inverses(refl_ref, keep):
    _, groups, block, window = refl_ref.shape
    wide = 2 * block
    groups = range(groups)
    firsts, seconds, sfirst, ssecond = [], [], [], []
    col = lax.broadcasted_iota(jnp.int32, (block, window), 1)
    for g in groups:
        a = refl_ref[0, g]
        b = jnp.where(keep | (col < block), refl_ref[1, g], 0.0)
        firsts.append(a)
        seconds.append(b)
        sfirst.append(a * (2.0 / jnp.sum(a * a, 1, keepdims=True)))
        ssecond.append(b * (2.0 / jnp.sum(b * b, 1, keepdims=True)))
    above = lax.broadcasted_iota(jnp.int32, (block, wide), 0) < (
        lax.broadcasted_iota(jnp.int32, (block, wide), 1) % block
    )
    near, cross = [], []
    for g in groups:
        ha = halves(firsts[g])
        gq = mm(ssecond[g], halves(seconds[g]), NT)
        gp = mm(sfirst[g], ha, NT)
        near.append(jnp.where(above, jnp.concatenate([gq, gp], 1), 0.0))
        cross.append(
            mm(ssecond[g][:, :block], (ha[0][:, block:], ha[1][:, block:]), NT)
        )

    def diagonal(value, size):
        mask = same_block((wide, wide), size, size, wide)
        return tuple(
            jnp.where(mask, jnp.concatenate([part] * (wide // size), 0), jnp.zeros((), BF16))
            for part in halves(value)
        )

    def gather_blocks(value, size):
        total = None
        for place in range(block // size):
            part = value[place * size : (place + 1) * size]
            pcol = lax.broadcasted_iota(jnp.int32, part.shape, 1)
            part = jnp.where((pcol % block) // size == place, part, 0.0)
            total = part if total is None else total + part
        return total

    def widen(value, size):
        old = value.shape[0]
        tall = jnp.concatenate([value] * (size // old), 0)
        return jnp.where(same_block(tall.shape, old, old, size), tall, 0.0)

    def quad(result, ring, size):
        across = [mm(r, diagonal(b, size)) for r, b in zip(result, ring)]
        halved = [halves(x) for x in across]
        once = [r - mm(x, diagonal(r, size)) for r, x in zip(result, halved)]
        square = [mm(h, diagonal(x, size)) for h, x in zip(halved, across)]
        return [o + mm(s, diagonal(o, size)) for o, s in zip(once, square)]

    small = [gather_blocks(n, 16) for n in near]
    shape = small[0].shape
    row = lax.broadcasted_iota(jnp.int32, shape, 0)
    scol = lax.broadcasted_iota(jnp.int32, shape, 1)
    eye = jnp.where(row == scol % 16, 1.0, 0.0)
    inner = (row // 4) == (scol % 16) // 4
    tiny = [jnp.where(inner, n, 0.0) for n in small]
    square = [mm(n, diagonal(n, 16)) for n in tiny]
    result = [eye - n for n in tiny]
    result = [r + mm(r, diagonal(s, 16)) for r, s in zip(result, square)]
    result = quad(result, [jnp.where(inner, 0.0, n) for n in small], 16)
    middle = [gather_blocks(n, 64) for n in near]
    mmask = same_block(middle[0].shape, 16, 16, 64)
    result = [widen(r, 64) for r in result]
    result = quad(result, [jnp.where(mmask, 0.0, n) for n in middle], 64)
    result = [widen(r, block) for r in result]
    bmask = same_block((block, wide), 64, 64, block)
    across = [mm(r, diagonal(jnp.where(bmask, 0.0, n), block)) for r, n in zip(result, near)]
    result = [r - mm(x, diagonal(r, block)) for r, x in zip(result, across)]
    return [
        (
            firsts[g],
            seconds[g],
            sfirst[g],
            ssecond[g],
            cross[g],
            result[g][:, :block],
            result[g][:, block:],
        )
        for g in groups
    ]


def joined(first, second):
    block = first.shape[0]
    none = jnp.zeros((block, block), F32)
    return jnp.concatenate(
        [jnp.concatenate([none, second], 1), jnp.concatenate([first, none], 1)], 0
    )


def whole_operator(parts, out_ref):
    first, second, sfirst, ssecond, cross, q, p = parts
    q, p = halves(q), halves(p)
    block = first.shape[0]
    link = mm(mm(q, cross), p)
    solved_p = mm(p, sfirst)
    solved_q = mm(q, ssecond)
    reach = mm(link, sfirst)
    none = jnp.zeros((block, block), F32)
    solved = jnp.concatenate(
        [
            jnp.concatenate(
                [-reach[:, :block], solved_q[:, :block] - reach[:, block:], solved_q[:, block:]], 1
            ),
            jnp.concatenate([solved_p, none], 1),
        ],
        0,
    )
    top = mm(first[:, :block], solved[block:, : 2 * block], TN)
    both = jnp.concatenate([second[:, :block], first[:, block:]], 0)
    moved = jnp.concatenate(
        [
            jnp.concatenate([top, none], 1),
            mm(both, solved, TN),
            mm(second[:, block:], solved[:block], TN),
        ],
        0,
    )
    row = lax.broadcasted_iota(jnp.int32, moved.shape, 0)
    col = lax.broadcasted_iota(jnp.int32, moved.shape, 1)
    out_ref[...] = jnp.where(row == col, 1.0, 0.0) - moved


def pair_action(parts, window):
    first, second, sfirst, ssecond, cross, q, p = parts
    q, p = halves(q), halves(p)
    block = first.shape[0]
    cols = window.shape[1]
    weights_p = jnp.concatenate([mm(sfirst, window[: 2 * block]), sfirst[:, :block]], 1)
    weights_q = mm(ssecond, window[block:])
    weights_q = jnp.concatenate([weights_q, jnp.zeros((block, block), F32)], 1)
    solved_p = mm(p, weights_p)
    solved_q = mm(q, weights_q - mm(cross, solved_p))
    moved = mm(joined(first, second), jnp.concatenate([solved_q, solved_p], 0), TN)
    row = lax.broadcasted_iota(jnp.int32, (3 * block, block), 0)
    col = lax.broadcasted_iota(jnp.int32, (3 * block, block), 1)
    return window - moved[:, :cols], jnp.where(row == col, 1.0, 0.0) - moved[:, cols:]


def pick_near(node, core, value):
    block = value.shape[0] // 3
    send_up = (core == 0) & ((node & 1) == 1)
    return jnp.where(send_up, value[:block], value[2 * block :])


def pick_far(node, value):
    block = value.shape[0] // 3
    return jnp.where((node & 2) == 0, value[2 * block :], value[:block])


def half_of(core, ref):
    rows = ref.shape[0] // PAIR
    return ref[pl.ds(pl.multiple_of(core * rows, rows), rows), :]


def first_kernel(count, nodes, place_ref, *refs):
    mine, theirs = refs[:count], refs[count : 2 * count]
    top_ref, low_ref, near_ref, far_ref = refs[2 * count : 2 * count + 4]
    (fixed_ref, lead_ref, out_near, out_far), keep_refs = refs[2 * count + 4 : 2 * count + 8], refs[2 * count + 8 : -1]
    refl_ref = refs[-1]
    block = top_ref.shape[0]
    node, core, vec = place_ref[0], place_ref[1], place_ref[2]
    groups, rows, _ = mine[0].shape
    for step in range(count):
        at = pl.ds(pl.multiple_of((step ^ vec) * rows, rows), rows)
        for group in range(groups):
            refl_ref[core, group, at, :] = mine[step][group]
            refl_ref[1 - core, group, at, :] = theirs[step][group]
    parts = pair_inverses(refl_ref, node != nodes - 1)
    below = jnp.where((node & 1) == 0, near_ref[...], far_ref[...])
    window = jnp.concatenate(
        [
            jnp.where(node == 0, top_ref[...], 0.0),
            low_ref[...],
            jnp.where(node == nodes - 1, 0.0, below),
        ],
        0,
    )
    fixed, lead = pair_action(parts[0], window)
    fixed_ref[...] = fixed
    lead_ref[...] = lead
    out_near[:block] = pick_near(node, core, fixed)
    out_near[block:] = pick_near(node, core, lead)
    out_far[...] = jnp.where(core == 0, pick_far(node, fixed), pick_far(node, lead))
    for group in range(1, groups):
        for part, array in enumerate(parts[group]):
            keep_refs[part][group - 1] = array


def later_kernel(place_ref, *refs):
    parts, (oper_ref, map_ref, map_half) = refs[:7], refs[7:]
    core = place_ref[1]
    later, size, _ = oper_ref.shape
    block = size // 3
    for group in range(later):
        whole_operator([part[group] for part in parts], oper_ref.at[group])
    if later != 2:
        return
    up, own, out = (slice(part * block, (part + 1) * block) for part in range(3))
    map_ref[:block] = oper_ref[0, out, :block]
    map_ref[block : 2 * block] = oper_ref[0, up, :block]
    map_ref[2 * block : 3 * block] = mm(oper_ref[1, out, own], oper_ref[0, own, :block])
    map_ref[3 * block : 4 * block] = oper_ref[1, out, out]
    map_ref[4 * block :] = oper_ref[1, out, :block]
    map_half[...] = half_of(core, map_ref)


def between_kernel(place_ref, fixed_ref, lead_ref, oper_ref, base_ref, onto_ref):
    block = fixed_ref.shape[0] // 3
    own = slice(block, 2 * block)
    first = jnp.where(place_ref[0] == 0, fixed_ref[:block], 0.0)
    operator = oper_ref.at[0]
    base = mm(operator[:, : 2 * block], jnp.concatenate([first, fixed_ref[own]], 0))
    onto = jnp.concatenate([operator[:, 2 * block :], mm(operator[:, own], lead_ref[own])], 1)
    rows = oper_ref[1, 2 * block :, : 2 * block]
    cols = base.shape[1]
    both = jnp.concatenate([base[: 2 * block], onto[: 2 * block]], 1)
    both = jnp.concatenate([jnp.where(place_ref[0] == 0, both[:block], 0.0), both[block:]], 0)
    both = mm(rows, both)
    base_ref[: 3 * block] = base
    base_ref[3 * block :] = both[:, :cols]
    onto_ref[: 3 * block] = onto
    onto_ref[3 * block :] = both[:, cols:]


def next_kernel(place_ref, near_ref, far_ref, near2_ref, far2_ref, fixed_ref, lead_ref, base_ref, onto_ref, *outs):
    out_fixed, out_vec, out_half = outs
    block = far_ref.shape[0]
    node, core = place_ref[0], place_ref[1]
    here = core == 0
    odd, high = (node & 1) == 1, (node & 2) == 2
    near, near2, far, far2 = near_ref[...], near2_ref[...], far_ref[...], far2_ref[...]
    came1, map1 = (jnp.where(here, near[at], near2[at]) for at in (slice(0, block), slice(block, None)))
    came2, map2 = (jnp.where(here, near2[at], near[at]) for at in (slice(0, block), slice(block, None)))
    came3, map3 = jnp.where(here, far, far2), jnp.where(here, far2, far)
    carry = jnp.where(high, jnp.where(odd, came3, came2), came1)
    carry = jnp.where(node == 0, 0.0, carry)
    step = jnp.where(odd, came2, came3) + mm(jnp.where(odd, map2, map3), carry)
    carry = jnp.where(high, step, carry)
    step = came1 + mm(map1, carry)
    carry = jnp.where(node == 3, step, carry)
    up, own, out = (slice(part * block, (part + 1) * block) for part in range(3))
    cols = carry.shape[1]
    reach = mm(
        jnp.where(odd, map3, map1), jnp.concatenate([fixed_ref[out], lead_ref[out]], 1)
    )
    below = jnp.where(odd, came3, came1) + reach[:, :cols] + mm(reach[:, cols:], carry)
    below = jnp.where(node == 3, 0.0, below)
    fixed = base_ref[...] + mm(onto_ref[...], jnp.concatenate([below, carry], 0))
    out_fixed[...] = fixed[: 3 * block]
    out_vec[:block] = fixed[out]
    out_vec[block : 2 * block] = fixed[up]
    out_vec[2 * block :] = fixed[3 * block :]
    out_half[...] = half_of(core, out_vec)


def last_kernel(place_ref, *refs):
    vecs, maps, (fixed_ref, oper_ref, out_ref) = refs[:5], refs[5:10], refs[10:]
    block = out_ref.shape[0]
    own, out = slice(block, 2 * block), slice(2 * block, 3 * block)
    here = place_ref[1] == 0

    def either(one_ref, two_ref, first, last):
        return jnp.where(here, one_ref[first:last], two_ref[first:last])

    def fetch(arrays, mask, part):
        near_ref, far_ref, near2_ref, far2_ref, own_ref = arrays
        first, last = part * block, (part + 1) * block
        if mask == 0:
            return own_ref[first:last]
        if mask == 1:
            return either(near_ref, near2_ref, first, last)
        if mask == 2:
            return either(near2_ref, near_ref, first, last)
        half = far_ref.shape[0]
        pieces = []
        if first < half:
            pieces.append(either(far_ref, far2_ref, first, min(last, half)))
        if last > half:
            pieces.append(either(far2_ref, far_ref, max(first, half) - half, last - half))
        return jnp.concatenate(pieces, 0)

    def finish(node):
        offset = lambda pair, part: fetch(vecs, node ^ pair, part)
        matrix = lambda pair, part: fetch(maps, node ^ pair, part)
        at = pl.ds(pl.multiple_of(place_ref[1] * block, block), block)
        reach = min(node + 1, 3)
        carries = [None]
        for pair in range(reach):
            carry = offset(pair, 0)
            if pair:
                carry = carry + mm(matrix(pair, 0), carries[pair])
            carries.append(carry)
        belows = [
            offset(pair + 1, 1) + mm(matrix(pair + 1, 1), carries[pair + 1])
            for pair in range(reach)
        ]
        final = None
        for pair in range(node):
            end = mm(matrix(pair, 3), belows[pair])
            if pair:
                end = end + mm(matrix(pair, 2), carries[pair]) + mm(matrix(pair, 4), final)
            final = offset(pair, 2) + end
        reached = fixed_ref[: 2 * block]
        if node:
            reached = reached + mm(oper_ref[0, : 2 * block, :block], carries[node])
        else:
            final = reached[:block]
        total = mm(oper_ref[1, at, own], reached[own])
        if node < 3:
            total = total + mm(oper_ref[1, at, out], belows[node])
        out_ref[...] = total + mm(oper_ref[1, at, :block], final)

    for node in range(4):
        pl.when(place_ref[0] == node)(functools.partial(finish, node))


def call(kernel, outs, operands, scratch=(), work=0):
    vmem = pl.BlockSpec(memory_space=pltpu.VMEM)
    return pl.pallas_call(
        kernel,
        out_shape=[jax.ShapeDtypeStruct(shape, F32) for shape in outs],
        in_specs=[pl.BlockSpec(memory_space=pltpu.SMEM)] + [vmem] * (len(operands) - 1),
        out_specs=[vmem] * len(outs),
        scratch_shapes=list(scratch),
        cost_estimate=pl.CostEstimate(flops=work, bytes_accessed=0, transcendentals=0),
        compiler_params=pltpu.CompilerParams(vmem_limit_bytes=16 << 20),
    )(*operands)


def dot(left, right):
    return jnp.matmul(left, right, precision=lax.Precision.HIGHEST)


def spread(value, axis, size):
    if size & (size - 1) or size > 8:
        gathered = lax.all_gather(value, axis)
        return [gathered[place] for place in range(size)], False
    return [value] + [
        lax.ppermute(value, axis, [(place, place ^ mask) for place in range(size)])
        for mask in range(1, size)
    ], True


def many_pairs(fixed, lead, operators, node, nodes, row_count):
    groups, block = 1 + operators.shape[0], fixed.shape[0] // 3
    members = [[place * PAIR + core for place in range(nodes)] for core in range(PAIR)]
    for group in range(groups):
        down = jnp.concatenate([fixed[2 * block :], lead[2 * block :]], 0)
        up = jnp.concatenate([fixed[:block], lead[:block]], 0)
        earlier = lax.all_gather(down, "rows", axis_index_groups=members)
        later = lax.ppermute(
            up, "rows", [(place, place - PAIR) for place in range(PAIR, row_count)]
        )
        carry = jnp.zeros((block, fixed.shape[1]), F32)
        for place in range(nodes - 1):
            step = earlier[place, :block] + dot(earlier[place, block:], carry)
            carry = jnp.where(node > place, step, carry)
        result = fixed + dot(lead, carry)
        if group < groups - 1:
            below = later[:block] + dot(later[block:], result[2 * block :])
            window = jnp.concatenate(
                [
                    jnp.where(node == 0, result[:block], 0.0),
                    result[block : 2 * block],
                    jnp.where(node == nodes - 1, 0.0, below),
                ],
                0,
            )
            lead = operators[group][:, :block]
            fixed = dot(operators[group], window)
    return result


def local(vectors, reflectors):
    groups, _, _, window = reflectors.shape
    block = window // 2
    cols = vectors.shape[1]
    row_index = lax.axis_index("rows")
    row_count = lax.axis_size("rows")
    vec_index = lax.axis_index("vecs")
    vec_count = lax.axis_size("vecs")
    nodes = row_count // PAIR
    node = row_index // PAIR
    core = row_index % PAIR

    def swap(value, masks):
        moves = [
            (place, ((place // PAIR) ^ masks[place % PAIR]) * PAIR + place % PAIR)
            for place in range(row_count)
        ]
        return lax.ppermute(value, "rows", moves)

    def across(value):
        return lax.ppermute(value, "rows", [(place, place ^ 1) for place in range(row_count)])

    mine, mixed = spread(reflectors[:, 0], "vecs", vec_count)
    other = across(vectors)
    top = jnp.where(core == 0, vectors, other)
    low = jnp.where(core == 0, other, vectors)
    if nodes == 4:
        below = [swap(top, (1, 1)), swap(top, (3, 3))]
    else:
        below = [
            lax.ppermute(
                top, "rows", [(place, place - PAIR) for place in range(PAIR, row_count)]
            )
        ] * 2
    theirs = [across(piece) for piece in mine]
    mine[0] = jnp.where(vec_index < 0, 0.0, mine[0])
    place = jnp.stack([node, core, vec_index if mixed else 0]).astype(jnp.int32)
    hold = lax.optimization_barrier
    later = groups - 1
    size = 3 * block
    maps = 5 * block
    fixed, lead, near, far, *parts = call(
        functools.partial(first_kernel, len(mine), nodes),
        [
            (size, cols),
            (size, block),
            (2 * block, cols),
            (block, cols),
            *[(later, block, window)] * 4,
            *[(later, block, block)] * 3,
        ],
        [place, *mine, *theirs, top, low, *below],
        [pltpu.VMEM((PAIR, groups, block, window), F32)],
    )
    operators, sent, sent_half = call(
        later_kernel,
        [(later, size, size), (maps, block), (maps // PAIR, block)],
        [place, *parts],
        work=32 * size**3,
    )
    if nodes != 4 or groups != 3:
        result = many_pairs(fixed, lead, operators, node, nodes, row_count)
        return jnp.where(core == 0, result[:block], result[block : 2 * block])

    def shared(near, far):
        return [place, near, far, across(near), across(far)]

    base, onto = call(
        between_kernel,
        [(4 * block, cols), (4 * block, 2 * block)],
        [place, fixed, lead, operators],
        work=32 * size**3,
    )
    near, far = swap(near, (1, 2)), swap(far, (3, 3))
    near, far, base = hold((near, far, base))
    known = [swap(sent, (1, 2)), swap(sent_half, (3, 3))]
    fixed, vec, vec_half = call(
        next_kernel,
        [(size, cols), (size, cols), (size // PAIR, cols)],
        [*shared(near, far), fixed, lead, base, onto],
    )
    near, far = swap(vec, (1, 2)), swap(vec_half, (3, 3))
    far, *known = hold((far, *known))
    far2, known2 = across(far), across(known[1])
    near, far2, known2 = hold((near, far2, known2))
    (result,) = call(
        last_kernel,
        [(block, cols)],
        [place, near, far, across(near), far2, vec, *known, across(known[0]), known2, sent, fixed, operators],
    )
    return result


def solution(mesh):
    placed = (P("rows", "vecs"), P(None, "rows", "vecs", None))
    return jax.shard_map(
        local, mesh=mesh, in_specs=placed, out_specs=P("rows", "vecs"), check_vma=False
    )
```

```python
import functools
import jax
import jax.numpy as jnp
from jax import lax
from jax.experimental import pallas as pl
from jax.experimental.pallas import tpu as pltpu
from jax.sharding import PartitionSpec as P

PAIR = 2
F32, BF16 = jnp.float32, jnp.bfloat16
NN = ((1,), (0,))
NT = ((1,), (1,))
TN = ((0,), (0,))


def halves(value):
    high = value.astype(BF16)
    return high, (value - high.astype(F32)).astype(BF16)


def mm(left, right, dims=NN):
    left = left if isinstance(left, tuple) else halves(left)
    right = right if isinstance(right, tuple) else halves(right)

    (lc,), (rc,) = dims
    return lax.dot_general(
        jnp.concatenate([left[0], left[0], left[1]], lc),
        jnp.concatenate([right[0], right[1], right[0]], rc),
        (dims, ((), ())),
        preferred_element_type=F32,
    )


def thirds(value):
    high, rest = halves(value)
    low = (value - high.astype(F32) - rest.astype(F32)).astype(BF16)
    return high, rest, low


def fine_mm(left, right, dims=NN):
    (a, b, c), (x, y, z) = thirds(left), thirds(right)
    (lc,), (rc,) = dims
    return lax.dot_general(
        jnp.concatenate([a, a, b, b, a, c], lc),
        jnp.concatenate([x, y, x, y, z, x], rc),
        (dims, ((), ())),
        preferred_element_type=F32,
    )


def same_block(shape, rows_block, cols_block, wrap):
    row = lax.broadcasted_iota(jnp.int32, shape, 0)
    col = lax.broadcasted_iota(jnp.int32, shape, 1)
    return (row // rows_block) == ((col % wrap) // cols_block)


def pair_inverses(refl_ref, keep):
    _, groups, block, window = refl_ref.shape
    wide = 2 * block
    groups = range(groups)
    firsts, seconds, sfirst, ssecond = [], [], [], []
    col = lax.broadcasted_iota(jnp.int32, (block, window), 1)
    for g in groups:
        a = refl_ref[0, g]
        b = jnp.where(keep | (col < block), refl_ref[1, g], 0.0)
        firsts.append(a)
        seconds.append(b)
        sfirst.append(a * (2.0 / jnp.sum(a * a, 1, keepdims=True)))
        ssecond.append(b * (2.0 / jnp.sum(b * b, 1, keepdims=True)))
    above = lax.broadcasted_iota(jnp.int32, (block, wide), 0) < (
        lax.broadcasted_iota(jnp.int32, (block, wide), 1) % block
    )
    near, cross = [], []
    for g in groups:
        gq = fine_mm(ssecond[g], seconds[g], NT)
        gp = fine_mm(sfirst[g], firsts[g], NT)
        near.append(jnp.where(above, jnp.concatenate([gq, gp], 1), 0.0))
        cross.append(
            fine_mm(ssecond[g][:, :block], firsts[g][:, block:], NT)
        )

    def diagonal(value, size):
        mask = same_block((wide, wide), size, size, wide)
        return tuple(
            jnp.where(mask, jnp.concatenate([part] * (wide // size), 0), jnp.zeros((), BF16))
            for part in halves(value)
        )

    def gather_blocks(value, size):
        total = None
        for place in range(block // size):
            part = value[place * size : (place + 1) * size]
            pcol = lax.broadcasted_iota(jnp.int32, part.shape, 1)
            part = jnp.where((pcol % block) // size == place, part, 0.0)
            total = part if total is None else total + part
        return total

    def widen(value, size):
        old = value.shape[0]
        tall = jnp.concatenate([value] * (size // old), 0)
        return jnp.where(same_block(tall.shape, old, old, size), tall, 0.0)

    def quad(result, ring, size):
        across = [mm(r, diagonal(b, size)) for r, b in zip(result, ring)]
        halved = [halves(x) for x in across]
        once = [r - mm(x, diagonal(r, size)) for r, x in zip(result, halved)]
        square = [mm(h, diagonal(x, size)) for h, x in zip(halved, across)]
        return [o + mm(s, diagonal(o, size)) for o, s in zip(once, square)]

    small = [gather_blocks(n, 16) for n in near]
    shape = small[0].shape
    row = lax.broadcasted_iota(jnp.int32, shape, 0)
    scol = lax.broadcasted_iota(jnp.int32, shape, 1)
    eye = jnp.where(row == scol % 16, 1.0, 0.0)
    inner = (row // 4) == (scol % 16) // 4
    tiny = [jnp.where(inner, n, 0.0) for n in small]
    square = [mm(n, diagonal(n, 16)) for n in tiny]
    result = [eye - n for n in tiny]
    result = [r + mm(r, diagonal(s, 16)) for r, s in zip(result, square)]
    result = quad(result, [jnp.where(inner, 0.0, n) for n in small], 16)
    middle = [gather_blocks(n, 64) for n in near]
    mmask = same_block(middle[0].shape, 16, 16, 64)
    result = [widen(r, 64) for r in result]
    result = quad(result, [jnp.where(mmask, 0.0, n) for n in middle], 64)
    result = [widen(r, block) for r in result]
    bmask = same_block((block, wide), 64, 64, block)
    across = [mm(r, diagonal(jnp.where(bmask, 0.0, n), block)) for r, n in zip(result, near)]
    result = [r - mm(x, diagonal(r, block)) for r, x in zip(result, across)]
    return [
        (
            firsts[g],
            seconds[g],
            sfirst[g],
            ssecond[g],
            cross[g],
            result[g][:, :block],
            result[g][:, block:],
        )
        for g in groups
    ]


def joined(first, second):
    block = first.shape[0]
    none = jnp.zeros((block, block), F32)
    return jnp.concatenate(
        [jnp.concatenate([none, second], 1), jnp.concatenate([first, none], 1)], 0
    )


def whole_operator(parts, out_ref):
    first, second, sfirst, ssecond, cross, q, p = parts
    q, p = halves(q), halves(p)
    block = first.shape[0]
    link = mm(mm(q, cross), p)
    solved_p = mm(p, sfirst)
    solved_q = mm(q, ssecond)
    reach = mm(link, sfirst)
    none = jnp.zeros((block, block), F32)
    solved = jnp.concatenate(
        [
            jnp.concatenate(
                [-reach[:, :block], solved_q[:, :block] - reach[:, block:], solved_q[:, block:]], 1
            ),
            jnp.concatenate([solved_p, none], 1),
        ],
        0,
    )
    top = mm(first[:, :block], solved[block:, : 2 * block], TN)
    both = jnp.concatenate([second[:, :block], first[:, block:]], 0)
    moved = jnp.concatenate(
        [
            jnp.concatenate([top, none], 1),
            mm(both, solved, TN),
            mm(second[:, block:], solved[:block], TN),
        ],
        0,
    )
    row = lax.broadcasted_iota(jnp.int32, moved.shape, 0)
    col = lax.broadcasted_iota(jnp.int32, moved.shape, 1)
    out_ref[...] = jnp.where(row == col, 1.0, 0.0) - moved


def pair_action(parts, window):
    first, second, sfirst, ssecond, cross, q, p = parts
    q, p = halves(q), halves(p)
    block = first.shape[0]
    cols = window.shape[1]
    weights_p = jnp.concatenate([mm(sfirst, window[: 2 * block]), sfirst[:, :block]], 1)
    weights_q = mm(ssecond, window[block:])
    weights_q = jnp.concatenate([weights_q, jnp.zeros((block, block), F32)], 1)
    solved_p = mm(p, weights_p)
    solved_q = mm(q, weights_q - mm(cross, solved_p))
    moved = mm(joined(first, second), jnp.concatenate([solved_q, solved_p], 0), TN)
    row = lax.broadcasted_iota(jnp.int32, (3 * block, block), 0)
    col = lax.broadcasted_iota(jnp.int32, (3 * block, block), 1)
    return window - moved[:, :cols], jnp.where(row == col, 1.0, 0.0) - moved[:, cols:]


def pick_near(node, core, value):
    block = value.shape[0] // 3
    send_up = (core == 0) & ((node & 1) == 1)
    return jnp.where(send_up, value[:block], value[2 * block :])


def pick_far(node, value):
    block = value.shape[0] // 3
    return jnp.where((node & 2) == 0, value[2 * block :], value[:block])


def half_of(core, ref):
    rows = ref.shape[0] // PAIR
    return ref[pl.ds(pl.multiple_of(core * rows, rows), rows), :]


def first_kernel(count, nodes, place_ref, *refs):
    mine, theirs = refs[:count], refs[count : 2 * count]
    top_ref, low_ref, near_ref, far_ref = refs[2 * count : 2 * count + 4]
    (fixed_ref, lead_ref, out_near, out_far), keep_refs = refs[2 * count + 4 : 2 * count + 8], refs[2 * count + 8 : -1]
    refl_ref = refs[-1]
    block = top_ref.shape[0]
    node, core, vec = place_ref[0], place_ref[1], place_ref[2]
    groups, rows, _ = mine[0].shape
    for step in range(count):
        at = pl.ds(pl.multiple_of((step ^ vec) * rows, rows), rows)
        for group in range(groups):
            refl_ref[core, group, at, :] = mine[step][group]
            refl_ref[1 - core, group, at, :] = theirs[step][group]
    parts = pair_inverses(refl_ref, node != nodes - 1)
    below = jnp.where((node & 1) == 0, near_ref[...], far_ref[...])
    window = jnp.concatenate(
        [
            jnp.where(node == 0, top_ref[...], 0.0),
            low_ref[...],
            jnp.where(node == nodes - 1, 0.0, below),
        ],
        0,
    )
    fixed, lead = pair_action(parts[0], window)
    fixed_ref[...] = fixed
    lead_ref[...] = lead
    out_near[:block] = pick_near(node, core, fixed)
    out_near[block:] = pick_near(node, core, lead)
    out_far[...] = jnp.where(core == 0, pick_far(node, fixed), pick_far(node, lead))
    for group in range(1, groups):
        for part, array in enumerate(parts[group]):
            keep_refs[part][group - 1] = array


def later_kernel(place_ref, *refs):
    parts, (oper_ref, map_ref, map_half) = refs[:7], refs[7:]
    core = place_ref[1]
    later, size, _ = oper_ref.shape
    block = size // 3
    for group in range(later):
        whole_operator([part[group] for part in parts], oper_ref.at[group])
    if later != 2:
        return
    up, own, out = (slice(part * block, (part + 1) * block) for part in range(3))
    map_ref[:block] = oper_ref[0, out, :block]
    map_ref[block : 2 * block] = oper_ref[0, up, :block]
    map_ref[2 * block : 3 * block] = mm(oper_ref[1, out, own], oper_ref[0, own, :block])
    map_ref[3 * block : 4 * block] = oper_ref[1, out, out]
    map_ref[4 * block :] = oper_ref[1, out, :block]
    map_half[...] = half_of(core, map_ref)


def between_kernel(place_ref, fixed_ref, lead_ref, oper_ref, base_ref, onto_ref):
    block = fixed_ref.shape[0] // 3
    own = slice(block, 2 * block)
    first = jnp.where(place_ref[0] == 0, fixed_ref[:block], 0.0)
    operator = oper_ref.at[0]
    base = mm(operator[:, : 2 * block], jnp.concatenate([first, fixed_ref[own]], 0))
    onto = jnp.concatenate([operator[:, 2 * block :], mm(operator[:, own], lead_ref[own])], 1)
    rows = oper_ref[1, 2 * block :, : 2 * block]
    cols = base.shape[1]
    both = jnp.concatenate([base[: 2 * block], onto[: 2 * block]], 1)
    both = jnp.concatenate([jnp.where(place_ref[0] == 0, both[:block], 0.0), both[block:]], 0)
    both = mm(rows, both)
    base_ref[: 3 * block] = base
    base_ref[3 * block :] = both[:, :cols]
    onto_ref[: 3 * block] = onto
    onto_ref[3 * block :] = both[:, cols:]


def next_kernel(place_ref, near_ref, far_ref, near2_ref, far2_ref, fixed_ref, lead_ref, base_ref, onto_ref, *outs):
    out_fixed, out_vec, out_half = outs
    block = far_ref.shape[0]
    node, core = place_ref[0], place_ref[1]
    here = core == 0
    odd, high = (node & 1) == 1, (node & 2) == 2
    near, near2, far, far2 = near_ref[...], near2_ref[...], far_ref[...], far2_ref[...]
    came1, map1 = (jnp.where(here, near[at], near2[at]) for at in (slice(0, block), slice(block, None)))
    came2, map2 = (jnp.where(here, near2[at], near[at]) for at in (slice(0, block), slice(block, None)))
    came3, map3 = jnp.where(here, far, far2), jnp.where(here, far2, far)
    carry = jnp.where(high, jnp.where(odd, came3, came2), came1)
    carry = jnp.where(node == 0, 0.0, carry)
    step = jnp.where(odd, came2, came3) + mm(jnp.where(odd, map2, map3), carry)
    carry = jnp.where(high, step, carry)
    step = came1 + mm(map1, carry)
    carry = jnp.where(node == 3, step, carry)
    up, own, out = (slice(part * block, (part + 1) * block) for part in range(3))
    cols = carry.shape[1]
    reach = mm(
        jnp.where(odd, map3, map1), jnp.concatenate([fixed_ref[out], lead_ref[out]], 1)
    )
    below = jnp.where(odd, came3, came1) + reach[:, :cols] + mm(reach[:, cols:], carry)
    below = jnp.where(node == 3, 0.0, below)
    fixed = base_ref[...] + mm(onto_ref[...], jnp.concatenate([below, carry], 0))
    out_fixed[...] = fixed[: 3 * block]
    out_vec[:block] = fixed[out]
    out_vec[block : 2 * block] = fixed[up]
    out_vec[2 * block :] = fixed[3 * block :]
    out_half[...] = half_of(core, out_vec)


def last_kernel(place_ref, *refs):
    vecs, maps, (fixed_ref, oper_ref, out_ref) = refs[:5], refs[5:10], refs[10:]
    block = out_ref.shape[0]
    own, out = slice(block, 2 * block), slice(2 * block, 3 * block)
    here = place_ref[1] == 0

    def either(one_ref, two_ref, first, last):
        return jnp.where(here, one_ref[first:last], two_ref[first:last])

    def fetch(arrays, mask, part):
        near_ref, far_ref, near2_ref, far2_ref, own_ref = arrays
        first, last = part * block, (part + 1) * block
        if mask == 0:
            return own_ref[first:last]
        if mask == 1:
            return either(near_ref, near2_ref, first, last)
        if mask == 2:
            return either(near2_ref, near_ref, first, last)
        half = far_ref.shape[0]
        pieces = []
        if first < half:
            pieces.append(either(far_ref, far2_ref, first, min(last, half)))
        if last > half:
            pieces.append(either(far2_ref, far_ref, max(first, half) - half, last - half))
        return jnp.concatenate(pieces, 0)

    def finish(node):
        offset = lambda pair, part: fetch(vecs, node ^ pair, part)
        matrix = lambda pair, part: fetch(maps, node ^ pair, part)
        at = pl.ds(pl.multiple_of(place_ref[1] * block, block), block)
        reach = min(node + 1, 3)
        carries = [None]
        for pair in range(reach):
            carry = offset(pair, 0)
            if pair:
                carry = carry + mm(matrix(pair, 0), carries[pair])
            carries.append(carry)
        belows = [
            offset(pair + 1, 1) + mm(matrix(pair + 1, 1), carries[pair + 1])
            for pair in range(reach)
        ]
        final = None
        for pair in range(node):
            end = mm(matrix(pair, 3), belows[pair])
            if pair:
                end = end + mm(matrix(pair, 2), carries[pair]) + mm(matrix(pair, 4), final)
            final = offset(pair, 2) + end
        reached = fixed_ref[: 2 * block]
        if node:
            reached = reached + mm(oper_ref[0, : 2 * block, :block], carries[node])
        else:
            final = reached[:block]
        total = mm(oper_ref[1, at, own], reached[own])
        if node < 3:
            total = total + mm(oper_ref[1, at, out], belows[node])
        out_ref[...] = total + mm(oper_ref[1, at, :block], final)

    for node in range(4):
        pl.when(place_ref[0] == node)(functools.partial(finish, node))


def call(kernel, outs, operands, scratch=(), work=0):
    vmem = pl.BlockSpec(memory_space=pltpu.VMEM)
    return pl.pallas_call(
        kernel,
        out_shape=[jax.ShapeDtypeStruct(shape, F32) for shape in outs],
        in_specs=[pl.BlockSpec(memory_space=pltpu.SMEM)] + [vmem] * (len(operands) - 1),
        out_specs=[vmem] * len(outs),
        scratch_shapes=list(scratch),
        cost_estimate=pl.CostEstimate(flops=work, bytes_accessed=0, transcendentals=0),
        compiler_params=pltpu.CompilerParams(vmem_limit_bytes=16 << 20),
    )(*operands)


def dot(left, right):
    return jnp.matmul(left, right, precision=lax.Precision.HIGHEST)


def spread(value, axis, size):
    if size & (size - 1) or size > 8:
        gathered = lax.all_gather(value, axis)
        return [gathered[place] for place in range(size)], False
    return [value] + [
        lax.ppermute(value, axis, [(place, place ^ mask) for place in range(size)])
        for mask in range(1, size)
    ], True


def many_pairs(fixed, lead, operators, node, nodes, row_count):
    groups, block = 1 + operators.shape[0], fixed.shape[0] // 3
    members = [[place * PAIR + core for place in range(nodes)] for core in range(PAIR)]
    for group in range(groups):
        down = jnp.concatenate([fixed[2 * block :], lead[2 * block :]], 0)
        up = jnp.concatenate([fixed[:block], lead[:block]], 0)
        earlier = lax.all_gather(down, "rows", axis_index_groups=members)
        later = lax.ppermute(
            up, "rows", [(place, place - PAIR) for place in range(PAIR, row_count)]
        )
        carry = jnp.zeros((block, fixed.shape[1]), F32)
        for place in range(nodes - 1):
            step = earlier[place, :block] + dot(earlier[place, block:], carry)
            carry = jnp.where(node > place, step, carry)
        result = fixed + dot(lead, carry)
        if group < groups - 1:
            below = later[:block] + dot(later[block:], result[2 * block :])
            window = jnp.concatenate(
                [
                    jnp.where(node == 0, result[:block], 0.0),
                    result[block : 2 * block],
                    jnp.where(node == nodes - 1, 0.0, below),
                ],
                0,
            )
            lead = operators[group][:, :block]
            fixed = dot(operators[group], window)
    return result


def local(vectors, reflectors):
    groups, _, _, window = reflectors.shape
    block = window // 2
    cols = vectors.shape[1]
    row_index = lax.axis_index("rows")
    row_count = lax.axis_size("rows")
    vec_index = lax.axis_index("vecs")
    vec_count = lax.axis_size("vecs")
    nodes = row_count // PAIR
    node = row_index // PAIR
    core = row_index % PAIR

    def swap(value, masks):
        moves = [
            (place, ((place // PAIR) ^ masks[place % PAIR]) * PAIR + place % PAIR)
            for place in range(row_count)
        ]
        return lax.ppermute(value, "rows", moves)

    def across(value):
        return lax.ppermute(value, "rows", [(place, place ^ 1) for place in range(row_count)])

    mine, mixed = spread(reflectors[:, 0], "vecs", vec_count)
    other = across(vectors)
    top = jnp.where(core == 0, vectors, other)
    low = jnp.where(core == 0, other, vectors)
    if nodes == 4:
        below = [swap(top, (1, 1)), swap(top, (3, 3))]
    else:
        below = [
            lax.ppermute(
                top, "rows", [(place, place - PAIR) for place in range(PAIR, row_count)]
            )
        ] * 2
    theirs = [across(piece) for piece in mine]
    mine[0] = jnp.where(vec_index < 0, 0.0, mine[0])
    place = jnp.stack([node, core, vec_index if mixed else 0]).astype(jnp.int32)
    hold = lax.optimization_barrier
    later = groups - 1
    size = 3 * block
    maps = 5 * block
    fixed, lead, near, far, *parts = call(
        functools.partial(first_kernel, len(mine), nodes),
        [
            (size, cols),
            (size, block),
            (2 * block, cols),
            (block, cols),
            *[(later, block, window)] * 4,
            *[(later, block, block)] * 3,
        ],
        [place, *mine, *theirs, top, low, *below],
        [pltpu.VMEM((PAIR, groups, block, window), F32)],
    )
    operators, sent, sent_half = call(
        later_kernel,
        [(later, size, size), (maps, block), (maps // PAIR, block)],
        [place, *parts],
        work=32 * size**3,
    )
    if nodes != 4 or groups != 3:
        result = many_pairs(fixed, lead, operators, node, nodes, row_count)
        return jnp.where(core == 0, result[:block], result[block : 2 * block])

    def shared(near, far):
        return [place, near, far, across(near), across(far)]

    base, onto = call(
        between_kernel,
        [(4 * block, cols), (4 * block, 2 * block)],
        [place, fixed, lead, operators],
        work=32 * size**3,
    )
    near, far = swap(near, (1, 2)), swap(far, (3, 3))
    near, far, base = hold((near, far, base))
    known = [swap(sent, (1, 2)), swap(sent_half, (3, 3))]
    fixed, vec, vec_half = call(
        next_kernel,
        [(size, cols), (size, cols), (size // PAIR, cols)],
        [*shared(near, far), fixed, lead, base, onto],
    )
    near, far = swap(vec, (1, 2)), swap(vec_half, (3, 3))
    far, *known = hold((far, *known))
    far2, known2 = across(far), across(known[1])
    near, far2, known2 = hold((near, far2, known2))
    (result,) = call(
        last_kernel,
        [(block, cols)],
        [place, near, far, across(near), far2, vec, *known, across(known[0]), known2, sent, fixed, operators],
    )
    return result


def solution(mesh):
    placed = (P("rows", "vecs"), P(None, "rows", "vecs", None))
    return jax.shard_map(
        local, mesh=mesh, in_specs=placed, out_specs=P("rows", "vecs"), check_vma=False
    )
```
